512 devices in a mesh: seq: 32 (over x, y, core), head: 16 (over z).
Axes of the slice: x: 4, y: 4, z: 16, core: 2. Of those that a mesh axis runs over, the one named last changes fastest.
Arguments:
- queries: bfloat16 [16384, 8192], P('seq', 'head'), may hold values from -6 to 6
- keys: bfloat16 [16384, 8192], P('seq', 'head'), may hold values from -6 to 6
- values: bfloat16 [16384, 8192], P('seq', 'head'), may hold values from -6 to 6
- gain: bfloat16 [8192], P('head'), may hold values from 0.25 to 1.75
- d_out: bfloat16 [16384, 8192], P('seq', 'head'), may hold values from -6 to 6
Outputs:
- normed: bfloat16 [16384, 8192], P('seq', 'head')
- d_queries: bfloat16 [16384, 8192], P('seq', 'head')
- d_keys: bfloat16 [16384, 8192], P('seq', 'head')
- d_values: bfloat16 [16384, 8192], P('seq', 'head')
The draws below stay inside these ranges and needn't reach their ends.
All inputs are finite; a program needn't handle non-finite values.
Results may differ from the reference program's by a relative error of at most 0.0051.
Values sent between devices are 32-bit elements; how exact they have to be, the bound alone decides.
A program may use at most 64 MiB of HBM per device.

```python
import jax
import jax.numpy as jnp
from jax import lax

DK = 128
HEADS = 64
TOK_DEV = 512
TOKENS = 16384


def shard_levels(key, extent, cuts, least, largest):
    def one(axis_at, shards_of):
        steps = jax.random.uniform(jax.random.fold_in(jax.random.fold_in(key, 6), axis_at), (shards_of,), jnp.float32, least / len(cuts), largest / len(cuts))
        return jnp.repeat(jnp.exp(steps), extent[axis_at] // shards_of).reshape((-1,) + (1,) * (len(extent) - axis_at - 1))

    loudness = one(*cuts[0])
    for cut in cuts[1:]:
        loudness = loudness * one(*cut)
    return loudness


def normal_values(stream_key, extent, spread, most, cuts=(), kind=jnp.bfloat16):
    values = spread * jax.random.normal(stream_key, extent, jnp.float32)
    if cuts:
        values = values * shard_levels(stream_key, extent, cuts, -0.22, 0.18)
    return jnp.clip(values, -most, most).astype(kind)


def setup_inputs(seed: int = 0) -> dict:
    seeds = jax.random.split(jax.random.key(seed), 6)
    return {
        "queries": normal_values(seeds[0], (TOKENS, HEADS * DK), 1.0, 6.0, ((0, 32), (1, 16))),
        "keys": normal_values(seeds[1], (TOKENS, HEADS * DK), 1.0, 6.0, ((0, 32), (1, 16))),
        "values": normal_values(seeds[2], (TOKENS, HEADS * DK), 1.0, 6.0, ((0, 32), (1, 16))),
        "gain": jnp.clip(1.0 + 0.15 * jax.random.normal(seeds[3], (HEADS * DK,), jnp.float32), 0.25, 1.75).astype(jnp.bfloat16),
        "d_out": normal_values(seeds[4], (TOKENS, HEADS * DK), 1.0, 6.0, ((0, 32), (1, 16))),
    }


def product(form, left, right):
    return jnp.einsum(form, left.astype(jnp.float32), right.astype(jnp.float32), precision=lax.Precision.HIGHEST)

def rounded(array):
    return lax.optimization_barrier(array.astype(jnp.bfloat16)).astype(jnp.float32)

def reference(queries, keys, values, gain, d_out):
    blocks = TOKENS // TOK_DEV

    def split(array):
        return array.astype(jnp.float32).reshape(blocks, TOK_DEV, HEADS, DK)
    qf = split(queries)
    kf = split(keys)
    vf = split(values)
    steps = jnp.arange(TOK_DEV)
    causal = (steps[:, None] >= steps[None, :]).astype(jnp.float32)

    def forward(state, block):
        qb, kb, vb = block
        scores = rounded(product('thd,shd->hts', qb, kb) * causal)
        attn = product('hts,she->the', scores, vb) + product('thd,hde->the', qb, state)
        return (state + product('shd,she->hde', kb, vb), (attn, state))
    start = jnp.zeros((HEADS, DK, DK), jnp.float32)
    _, (attn, prevs) = lax.scan(forward, start, (qf, kf, vf))
    flat = attn.reshape(TOKENS, HEADS * DK)
    rms = jnp.sqrt(lax.optimization_barrier(jnp.mean(flat * flat, axis=1)) + 1e-05)
    gainf = gain.astype(jnp.float32)
    normed = (flat / rms[:, None] * gainf).astype(jnp.bfloat16)
    grad = d_out.astype(jnp.float32) * gainf
    inner = lax.optimization_barrier(jnp.mean(grad * flat, axis=1))
    d_attn = (grad - flat * (inner / (rms * rms))[:, None]) / rms[:, None]
    dsplit = rounded(d_attn).reshape(blocks, TOK_DEV, HEADS, DK)

    def backward(later, block):
        qb, kb, vb, db, prev = block
        scores = rounded(product('thd,shd->hts', qb, kb) * causal)
        d_scores = rounded(product('the,she->hts', db, vb) * causal)
        dq = product('hts,shd->thd', d_scores, kb) + product('the,hde->thd', db, prev)
        dk = product('hts,thd->shd', d_scores, qb) + product('she,hde->shd', vb, later)
        dv = product('hts,the->she', scores, db) + product('shd,hde->she', kb, later)
        return (later + product('thd,the->hde', qb, db), (dq, dk, dv))
    _, (dq, dk, dv) = lax.scan(backward, start, (qf, kf, vf, dsplit, prevs), reverse=True)
    shape = (TOKENS, HEADS * DK)
    return (normed, dq.reshape(shape).astype(jnp.bfloat16), dk.reshape(shape).astype(jnp.bfloat16), dv.reshape(shape).astype(jnp.bfloat16))
```

```python
import functools

import jax
import jax.numpy as jnp
from jax import lax
from jax.experimental import pallas as pl
from jax.experimental.pallas import tpu as pltpu
from jax.sharding import PartitionSpec as P

DK = 128
ROWS = 512
HEADS_HERE = 4
FEATURES = 8192
SIDE = 4
DEPTH = 16
MESH = pl.DeviceIdType.MESH
F32 = jnp.float32
BF16 = jnp.bfloat16

NN = (((1,), (0,)), ((), ()))
NT = (((1,), (1,)), ((), ()))
TN = (((0,), (0,)), ((), ()))


def dot(left, right, dims):
    return lax.dot_general(left, right, dims, preferred_element_type=F32)


def head(h):
    return pl.ds(h * DK, DK)


def halves(state, axis):
    high = state.astype(BF16)
    low = (state - high.astype(F32)).astype(BF16)
    return jnp.concatenate([high, low], axis=axis)


def body(
    q_hbm, k_hbm, v_hbm, gain_ref, d_hbm,
    normed_hbm, dq_hbm, dk_hbm, dv_hbm,
    q, k, v, d, normed, dq, dk, dv,
    qt, scores_t, attn, g, e, dk_part, dv_part,
    own, sib, chip, recv1, row, cols, recv2, pref,
    zsend, zrecv,
    load_sem, store_sem, send_sem, recv_sem, zsend_sem, zrecv_sem,
):
    s = lax.axis_index("seq")
    z = lax.axis_index("head")
    x, y, c = s // 8, (s // 2) % SIDE, s % 2
    sibling = (s + 1 - 2 * c, z)

    def along_y(step):
        return (x * 8 + ((y + step) % SIDE) * 2 + c, z)

    def along_x(step):
        return (((x + step) % SIDE) * 8 + y * 2 + c, z)

    def along_z(step):
        return (s, (z + step) % DEPTH)

    loads = [
        pltpu.make_async_copy(src, dst, load_sem.at[i])
        for i, (src, dst) in enumerate(((k_hbm, k), (v_hbm, v), (q_hbm, q), (d_hbm, d)))
    ]
    for load in loads:
        load.start()

    barrier = pltpu.get_barrier_semaphore()
    partners = [sibling]
    partners += [along_y(i) for i in range(1, SIDE)] + [along_x(i) for i in range(1, SIDE)]
    partners += [along_z(i) for i in range(1, DEPTH)]
    for partner in partners:
        pl.semaphore_signal(barrier, inc=1, device_id=partner, device_id_type=MESH)

    def message(way, number):
        here, there = pl.ds(256 * c, 256), pl.ds(256 * (1 - c), 256)
        if number == 0:
            src, dst, device = own.at[way, there], sib.at[way, 0], sibling
        elif number == 1:
            src, dst, device = own.at[way, here], sib.at[way, 1], sibling
        elif number == 2:
            src, dst, device = pref.at[way, here], pref.at[way, here], sibling
        elif number < 6:
            step = number - 2
            src, dst, device = chip.at[way, pl.ds(0, 128)], recv1.at[way, 0, step - 1], along_y(step)
        elif number < 9:
            step = number - 5
            src, dst, device = chip.at[way, pl.ds(128, 128)], recv1.at[way, 1, step - 1], along_x(step)
        elif number < 12:
            step = number - 8
            src, dst, device = row.at[way], recv2.at[way, 0, step - 1], along_x(step)
        else:
            step = number - 11
            wrapped = (y + step) // SIDE
            pick = 1 - wrapped if way == 0 else wrapped
            src, dst, device = cols.at[way, pick], recv2.at[way, 1, step - 1], along_y(step)
        return pltpu.make_async_remote_copy(
            src_ref=src, dst_ref=dst, send_sem=send_sem.at[way, number], recv_sem=recv_sem.at[way, number],
            device_id=device, device_id_type=MESH,
        )

    def zmessage(step):
        return pltpu.make_async_remote_copy(
            src_ref=zsend, dst_ref=zrecv.at[step - 1], send_sem=zsend_sem.at[step - 1],
            recv_sem=zrecv_sem.at[step - 1], device_id=along_z(step), device_id_type=MESH,
        )

    def counts(way, step, place):
        return step <= place if way == 0 else step > place

    def start_pair(way):
        message(way, 0).start()
        message(way, 1).start()

    def start_first(way):
        message(way, 0).wait_recv()
        chip[way] = own[way, pl.ds(256 * c, 256)] + sib[way, 0]
        for number in (4, 7, 3, 5, 6, 8):
            message(way, number).start()

    def start_second(way):
        for number in range(3, 9):
            message(way, number).wait_recv()
        mine = chip[way, pl.ds(0, 128)]
        total, before = mine, jnp.zeros_like(mine)
        for step in range(1, SIDE):
            block = recv1[way, 0, step - 1]
            total = total + block
            before = before + jnp.where(counts(way, step, y), block, 0.0)
        row[way] = total
        pref[way, pl.ds(256 * c, 128)] = before
        column = jnp.zeros_like(mine)
        for step in range(1, SIDE):
            column = column + jnp.where(counts(way, step, x), recv1[way, 1, step - 1], 0.0)
        cols[way, 0] = column
        cols[way, 1] = column + chip[way, pl.ds(128, 128)]
        for number in (10, 13, 9, 11, 12, 14):
            message(way, number).start()

    def start_third(way):
        for number in range(9, 15):
            message(way, number).wait_recv()
        first = pref[way, pl.ds(256 * c, 128)]
        second = cols[way, 0]
        for step in range(1, SIDE):
            first = first + jnp.where(counts(way, step, x), recv2[way, 0, step - 1], 0.0)
            second = second + recv2[way, 1, step - 1]
        pref[way, pl.ds(256 * c, 128)] = first
        pref[way, pl.ds(256 * c + 128, 128)] = second
        message(way, 2).start()
        message(way, 1).wait_recv()

    def state(way, h):
        half = h // 2
        other = (half + c) % 2
        add = c == 1 if way == 0 else c == 0
        block = sib[way, other, pl.ds((h % 2) * DK, DK)]
        return pref[way, pl.ds(h * DK, DK)] + jnp.where(add, block, 0.0)

    steps0 = lax.broadcasted_iota(jnp.int32, (DK, DK), 0)
    steps1 = lax.broadcasted_iota(jnp.int32, (DK, DK), 1)

    def causal(block, lower):
        keep = steps0 >= steps1 if lower else steps0 <= steps1
        if block.shape[1] == DK:
            return jnp.where(keep, block, 0.0).astype(BF16)
        if lower:
            cut = block.shape[1] - DK
            return jnp.concatenate(
                [block[:, :cut].astype(BF16), jnp.where(keep, block[:, cut:], 0.0).astype(BF16)], axis=1
            )
        return jnp.concatenate(
            [jnp.where(keep, block[:, :DK], 0.0).astype(BF16), block[:, DK:].astype(BF16)], axis=1
        )

    loads[0].wait()
    loads[1].wait()
    for h in range(HEADS_HERE):
        own[0, head(h)] = dot(k[:, head(h)], v[:, head(h)], TN)
    pl.semaphore_wait(barrier, len(partners))
    start_pair(0)
    loads[2].wait()
    loads[3].wait()

    start_first(0)

    def inner(h, carry):
        at = pl.ds(pl.multiple_of(h * DK, DK), DK)
        for r in range(4):
            strip = causal(dot(q[pl.ds(r * DK, DK), at], k[pl.ds(0, (r + 1) * DK), at], NT), True)
            attn[pl.ds(r * DK, DK), at] = dot(strip, v[pl.ds(0, (r + 1) * DK), at], NN)
        return carry

    lax.fori_loop(0, HEADS_HERE, inner, 0)
    start_second(0)

    def prepare(h, carry):
        at = pl.ds(pl.multiple_of(h * DK, DK), DK)
        qt[at, :] = q[:, at].astype(F32).T.astype(BF16)
        g[:, at] = d[:, at].astype(F32) * gain_ref[:, at]
        for r in range(4):
            rest = ROWS - r * DK
            strip = dot(k[pl.ds(r * DK, DK), at], q[pl.ds(r * DK, rest), at], NT)
            scores_t[h, pl.ds(r * DK, DK), pl.ds(r * DK, rest)] = causal(strip, False)
        return carry

    lax.fori_loop(0, HEADS_HERE, prepare, 0)
    start_third(0)
    message(0, 2).wait_recv()

    squares = jnp.zeros((ROWS, DK), F32)
    products = jnp.zeros((ROWS, DK), F32)
    for h in range(HEADS_HERE):
        qh = q[:, head(h)]
        total = attn[:, head(h)] + dot(jnp.concatenate([qh, qh], axis=1), halves(state(0, h), 0), NN)
        attn[:, head(h)] = total
        squares = squares + total * total
        products = products + total * g[:, head(h)]

    ones = jnp.ones((8, 3 * DK), BF16)

    def row_sums(array):
        high = array.astype(BF16)
        rest = array - high.astype(F32)
        middle = rest.astype(BF16)
        low = (rest - middle.astype(F32)).astype(BF16)
        return dot(ones, jnp.concatenate([high, middle, low], axis=1), NT)

    for i, array in enumerate((squares, products)):
        sums = row_sums(array)
        for j in range(4):
            zsend[pl.ds(4 * i + j, 1), :] = sums[0:1, j * DK : (j + 1) * DK]
    for step in (8, 7, 9, 6, 10, 5, 11, 4, 12, 3, 13, 2, 14, 1, 15):
        zmessage(step).start()

    totals = zsend[...]
    for step in range(1, DEPTH):
        zmessage(step).wait_recv()
    for step in range(1, DEPTH):
        totals = totals + zrecv[step - 1]
    means = totals / FEATURES
    rms = jnp.sqrt(means[0:4] + 1e-05)
    inverse = 1.0 / rms
    weight = means[4:8] * inverse * inverse
    columns = jnp.concatenate([inverse, weight], axis=0).T
    for j in range(4):
        at = pl.ds(j * DK, DK)
        delta = (g[at, :] - attn[at, :] * columns[:, 4 + j : 5 + j]) * columns[:, j : j + 1]
        e[at, :] = delta.astype(BF16)

    for h in range(HEADS_HERE):
        own[1, head(h)] = dot(qt[head(h), :], e[:, head(h)], NN)
    start_pair(1)
    for j in range(4):
        at = pl.ds(j * DK, DK)
        normed[at, :] = (attn[at, :] * columns[:, j : j + 1] * gain_ref[...]).astype(BF16)
    start_first(1)
    stores = [
        pltpu.make_async_copy(src, dst, store_sem.at[i])
        for i, (src, dst) in enumerate(((normed, normed_hbm), (dq, dq_hbm), (dk, dk_hbm), (dv, dv_hbm)))
    ]
    stores[0].start()

    def outer(h, carry):
        at = pl.ds(pl.multiple_of(h * DK, DK), DK)
        for r in range(4):
            low, rest = pl.ds(r * DK, DK), ROWS - r * DK
            strip = causal(dot(v[low, at], e[pl.ds(r * DK, rest), at], NT), False)
            dk_part[low, at] = dot(strip, q[pl.ds(r * DK, rest), at], NN)
            dv_part[low, at] = dot(scores_t[h, low, pl.ds(r * DK, rest)], e[pl.ds(r * DK, rest), at], NN)
        return carry

    lax.fori_loop(0, HEADS_HERE, outer, 0)
    start_second(1)

    for h in range(HEADS_HERE):
        back = halves(state(0, h), 1)
        for r in range(4):
            low = pl.ds(r * DK, DK)
            eh = e[low, head(h)]
            strip = causal(dot(eh, v[pl.ds(0, (r + 1) * DK), head(h)], NT), True)
            total = dot(strip, k[pl.ds(0, (r + 1) * DK), head(h)], NN)
            dq[low, head(h)] = (total + dot(jnp.concatenate([eh, eh], axis=1), back, NT)).astype(BF16)
    stores[1].start()
    start_third(1)
    message(1, 2).wait_recv()

    for h in range(HEADS_HERE):
        later = state(1, h)
        vh, kh = v[:, head(h)], k[:, head(h)]
        total = dk_part[:, head(h)] + dot(jnp.concatenate([vh, vh], axis=1), halves(later, 1), NT)
        dk[:, head(h)] = total.astype(BF16)
        total = dv_part[:, head(h)] + dot(jnp.concatenate([kh, kh], axis=1), halves(later, 0), NN)
        dv[:, head(h)] = total.astype(BF16)
    stores[2].start()
    stores[3].start()
    for way in range(2):
        for number in range(15):
            message(way, number).wait_send()
    for step in range(1, DEPTH):
        zmessage(step).wait_send()
    for store in stores:
        store.wait()


def shards(queries, keys, values, gain, d_out):
    whole = jax.ShapeDtypeStruct((ROWS, HEADS_HERE * DK), BF16)
    block = pltpu.VMEM((ROWS, HEADS_HERE * DK), BF16)
    wide = pltpu.VMEM((ROWS, HEADS_HERE * DK), F32)
    square = (DK, DK)
    anywhere = pl.BlockSpec(memory_space=pl.ANY)
    return pl.pallas_call(
        body,
        out_shape=[whole] * 4,
        in_specs=[anywhere, anywhere, anywhere, pl.BlockSpec(memory_space=pltpu.VMEM), anywhere],
        out_specs=[anywhere] * 4,
        scratch_shapes=[block] * 8
        + [
            pltpu.VMEM((HEADS_HERE * DK, ROWS), BF16),
            pltpu.VMEM((HEADS_HERE, ROWS, ROWS), BF16),
            wide, wide, block, wide, wide,
            pltpu.VMEM((2, 512, DK), F32),
            pltpu.VMEM((2, 2, 256, DK), F32),
            pltpu.VMEM((2, 256, DK), F32),
            pltpu.VMEM((2, 2, 3) + square, F32),
            pltpu.VMEM((2,) + square, F32),
            pltpu.VMEM((2, 2) + square, F32),
            pltpu.VMEM((2, 2, 3) + square, F32),
            pltpu.VMEM((2, 512, DK), F32),
            pltpu.VMEM((8, DK), F32),
            pltpu.VMEM((DEPTH - 1, 8, DK), F32),
            pltpu.SemaphoreType.DMA((4,)),
            pltpu.SemaphoreType.DMA((4,)),
            pltpu.SemaphoreType.DMA((2, 15)),
            pltpu.SemaphoreType.DMA((2, 15)),
            pltpu.SemaphoreType.DMA((DEPTH - 1,)),
            pltpu.SemaphoreType.DMA((DEPTH - 1,)),
        ],
        compiler_params=pltpu.CompilerParams(
            collective_id=0, has_side_effects=True, vmem_limit_bytes=32 * 1024 * 1024
        ),
        name="attention",
    )(queries, keys, values, gain.astype(F32).reshape(1, HEADS_HERE * DK), d_out)


def solution(mesh):
    in_specs = (P("seq", "head"), P("seq", "head"), P("seq", "head"), P("head"), P("seq", "head"))
    out_specs = (P("seq", "head"), P("seq", "head"), P("seq", "head"), P("seq", "head"))
    return jax.shard_map(shards, mesh=mesh, in_specs=in_specs, out_specs=out_specs, check_vma=False)
```

```python
import functools

import jax
import jax.numpy as jnp
from jax import lax
from jax.experimental import pallas as pl
from jax.experimental.pallas import tpu as pltpu
from jax.sharding import PartitionSpec as P

DK = 128
ROWS = 512
HEADS_HERE = 4
FEATURES = 8192
SIDE = 4
DEPTH = 16
MESH = pl.DeviceIdType.MESH
F32 = jnp.float32
BF16 = jnp.bfloat16

NN = (((1,), (0,)), ((), ()))
NT = (((1,), (1,)), ((), ()))
TN = (((0,), (0,)), ((), ()))


def dot(left, right, dims):
    return lax.dot_general(left, right, dims, preferred_element_type=F32)


def head(h):
    return pl.ds(h * DK, DK)


def halves(state, axis):
    high = state.astype(BF16)
    low = (state - high.astype(F32)).astype(BF16)
    return jnp.concatenate([high, low], axis=axis)


def body(
    q_hbm, k_hbm, v_hbm, gain_hbm, d_hbm,
    normed, dq, dk_part, dv_part, later, k, v,
    q, d, gain,
    qt, scores_t, attn, g, e,
    own, sib, chip, recv1, row, cols, recv2, pref,
    zsend, zrecv,
    load_sem, send_sem, recv_sem, zsend_sem, zrecv_sem, near_sem,
):
    s = lax.axis_index("seq")
    z = lax.axis_index("head")
    x, y, c = s // 8, (s // 2) % SIDE, s % 2
    sibling = (s + 1 - 2 * c, z)

    def along_y(step):
        return (x * 8 + ((y + step) % SIDE) * 2 + c, z)

    def along_x(step):
        return (((x + step) % SIDE) * 8 + y * 2 + c, z)

    def along_z(step):
        return (s, (z + step) % DEPTH)

    loads = [
        pltpu.make_async_copy(src, dst, load_sem.at[i])
        for i, (src, dst) in enumerate(((k_hbm, k), (v_hbm, v), (q_hbm, q), (d_hbm, d), (gain_hbm, gain)))
    ]
    for load in loads:
        load.start()

    barrier = pltpu.get_barrier_semaphore()
    partners = [sibling, along_z(1), along_z(DEPTH - 1)]
    partners += [along_y(i) for i in range(1, SIDE)] + [along_x(i) for i in range(1, SIDE)]
    for partner in partners:
        pl.semaphore_signal(barrier, inc=1, device_id=partner, device_id_type=MESH)

    def tell(turn):
        for step in (2**turn, DEPTH - 2**turn):
            pl.semaphore_signal(near_sem.at[turn], inc=1, device_id=along_z(step), device_id_type=MESH)

    def hear(turn):
        pl.semaphore_wait(near_sem.at[turn], 2)

    def half_head(half, j):
        return pl.ds(pl.multiple_of((2 * half + j) * DK, DK), DK)

    def message(way, number, src, dst, device):
        return pltpu.make_async_remote_copy(
            src_ref=src, dst_ref=dst, send_sem=send_sem.at[way, number], recv_sem=recv_sem.at[way, number],
            device_id=device, device_id_type=MESH,
        )

    def sib_message(way, j):
        if j == 2:
            return message(way, 2, own.at[way, pl.ds(256 * c, 256)], sib.at[way, 1], sibling)
        return message(way, j, own.at[way, half_head(1 - c, j)], sib.at[way, 0, pl.ds(j * DK, DK)], sibling)

    def pref_message(way, j):
        return message(way, 3 + j, pref.at[way, half_head(c, j)], pref.at[way, half_head(c, j)], sibling)

    def plane_message(way, phase, j, a, step):
        number = 5 + ((phase * 2 + j) * 2 + a) * 3 + step - 1
        device = along_y(step) if phase == a else along_x(step)
        if phase == 0:
            src, dst = chip.at[way, j, a], recv1.at[way, j, a, step - 1]
        elif a == 0:
            src, dst = row.at[way, j], recv2.at[way, j, a, step - 1]
        else:
            wrapped = (y + step) // SIDE
            pick = 1 - wrapped if way == 0 else wrapped
            src, dst = cols.at[way, j, pick], recv2.at[way, j, a, step - 1]
        return message(way, number, src, dst, device)

    def zmessage(step):
        return pltpu.make_async_remote_copy(
            src_ref=zsend, dst_ref=zrecv.at[step - 1], send_sem=zsend_sem.at[step - 1],
            recv_sem=zrecv_sem.at[step - 1], device_id=along_z(step), device_id_type=MESH,
        )

    def counts(way, step, place):
        return step <= place if way == 0 else step > place

    def start_first(way):
        for j in range(2):
            sib_message(way, j).wait_recv()
            total = own[way, half_head(c, j)] + sib[way, 0, pl.ds(j * DK, DK)]
            for a in range(2):
                chip[way, j, a] = total[64 * a : 64 * a + 64]
            for step in (2, 1, 3):
                for a in range(2):
                    plane_message(way, 0, j, a, step).start()

    def start_second(way):
        for j in range(2):
            for a in range(2):
                for step in range(1, SIDE):
                    plane_message(way, 0, j, a, step).wait_recv()
                mine = chip[way, j, a]
                if a == 0:
                    total, before = mine, jnp.zeros_like(mine)
                    for step in range(1, SIDE):
                        block = recv1[way, j, a, step - 1]
                        total = total + block
                        before = before + jnp.where(counts(way, step, y), block, 0.0)
                    row[way, j] = total
                    pref[way, pl.ds(256 * c + j * DK, 64)] = before
                else:
                    column = jnp.zeros_like(mine)
                    for step in range(1, SIDE):
                        column = column + jnp.where(counts(way, step, x), recv1[way, j, a, step - 1], 0.0)
                    cols[way, j, 0] = column
                    cols[way, j, 1] = column + mine
                for step in (2, 1, 3):
                    plane_message(way, 1, j, a, step).start()

    def start_third(way):
        for j in range(2):
            for a in range(2):
                for step in range(1, SIDE):
                    plane_message(way, 1, j, a, step).wait_recv()
                at = pl.ds(256 * c + j * DK + 64 * a, 64)
                if a == 0:
                    total = pref[way, at]
                    for step in range(1, SIDE):
                        total = total + jnp.where(counts(way, step, x), recv2[way, j, a, step - 1], 0.0)
                else:
                    total = cols[way, j, 0]
                    for step in range(1, SIDE):
                        total = total + recv2[way, j, a, step - 1]
                pref[way, at] = total
            pref_message(way, j).start()

    def state(way, mine, j):
        add = c == 1 if way == 0 else c == 0
        block = sib[way, 0 if mine else 1, pl.ds(j * DK, DK)]
        return pref[way, half_head(c if mine else 1 - c, j)] + jnp.where(add, block, 0.0)

    steps0 = lax.broadcasted_iota(jnp.int32, (DK, DK), 0)
    steps1 = lax.broadcasted_iota(jnp.int32, (DK, DK), 1)

    def causal(block, lower):
        keep = steps0 >= steps1 if lower else steps0 <= steps1
        if block.shape[1] == DK:
            return jnp.where(keep, block, 0.0).astype(BF16)
        if lower:
            cut = block.shape[1] - DK
            return jnp.concatenate(
                [block[:, :cut].astype(BF16), jnp.where(keep, block[:, cut:], 0.0).astype(BF16)], axis=1
            )
        return jnp.concatenate(
            [jnp.where(keep, block[:, :DK], 0.0).astype(BF16), block[:, DK:].astype(BF16)], axis=1
        )

    loads[0].wait()
    loads[1].wait()
    for j in range(2):
        at = half_head(1 - c, j)
        own[0, at] = dot(k[:, at], v[:, at], TN)
    pl.semaphore_wait(barrier, len(partners))
    tell(0)
    for j in range(2):
        sib_message(0, j).start()
    for j in range(2):
        at = half_head(c, j)
        own[0, at] = dot(k[:, at], v[:, at], TN)
    sib_message(0, 2).start()
    loads[2].wait()
    loads[3].wait()
    loads[4].wait()
    start_first(0)

    def inner(h, carry):
        at = pl.ds(pl.multiple_of(h * DK, DK), DK)
        for r in range(4):
            strip = causal(dot(q[pl.ds(r * DK, DK), at], k[pl.ds(0, (r + 1) * DK), at], NT), True)
            attn[pl.ds(r * DK, DK), at] = dot(strip, v[pl.ds(0, (r + 1) * DK), at], NN)
        return carry

    lax.fori_loop(0, HEADS_HERE, inner, 0)
    hear(0)
    tell(1)
    start_second(0)

    gains = gain[...].astype(F32)

    def prepare(h, carry):
        at = pl.ds(pl.multiple_of(h * DK, DK), DK)
        qt[at, :] = q[:, at].astype(F32).T.astype(BF16)
        for r in range(4):
            rest = ROWS - r * DK
            strip = dot(k[pl.ds(r * DK, DK), at], q[pl.ds(r * DK, rest), at], NT)
            scores_t[h, pl.ds(r * DK, DK), pl.ds(r * DK, rest)] = causal(strip, False)
        return carry

    lax.fori_loop(0, HEADS_HERE, prepare, 0)
    g[...] = d[...].astype(F32) * gains
    hear(1)
    tell(2)
    start_third(0)
    sib_message(0, 2).wait_recv()

    squares = jnp.zeros((ROWS, DK), F32)
    products = jnp.zeros((ROWS, DK), F32)
    for mine in (True, False):
        for j in range(2):
            if not mine:
                pref_message(0, j).wait_recv()
            at = half_head(c if mine else 1 - c, j)
            qh = q[:, at]
            total = attn[:, at] + dot(jnp.concatenate([qh, qh], axis=1), halves(state(0, mine, j), 0), NN)
            attn[:, at] = total
            squares = squares + total * total
            products = products + total * g[:, at]

    ones = jnp.ones((8, 3 * DK), BF16)

    def row_sums(array):
        high = array.astype(BF16)
        rest = array - high.astype(F32)
        middle = rest.astype(BF16)
        low = (rest - middle.astype(F32)).astype(BF16)
        return dot(ones, jnp.concatenate([high, middle, low], axis=1), NT)

    for i, array in enumerate((squares, products)):
        sums = row_sums(array)
        for j in range(4):
            zsend[pl.ds(4 * i + j, 1), :] = sums[0:1, j * DK : (j + 1) * DK]
    hear(2)
    for step in (8, 7, 9, 6, 10, 5, 11, 4, 12, 3, 13, 2, 14, 1, 15):
        zmessage(step).start()

    totals = zsend[...]
    for step in (1, 15, 2, 14, 3, 13, 4, 12, 5, 11, 6, 10, 7, 9, 8):
        zmessage(step).wait_recv()
        totals = totals + zrecv[step - 1]
    means = totals / FEATURES
    rms = jnp.sqrt(means[0:4] + 1e-05)
    inverse = 1.0 / rms
    weight = means[4:8] * inverse * inverse
    columns = jnp.concatenate([inverse, weight], axis=0).T
    for j in range(4):
        at = pl.ds(j * DK, DK)
        delta = (g[at, :] - attn[at, :] * columns[:, 4 + j : 5 + j]) * columns[:, j : j + 1]
        e[at, :] = delta.astype(BF16)

    for mine in (False, True):
        for j in range(2):
            at = half_head(c if mine else 1 - c, j)
            own[1, at] = dot(qt[at, :], e[:, at], NN)
            if not mine:
                sib_message(1, j).start()
    sib_message(1, 2).start()
    start_first(1)
    for j in range(4):
        at = pl.ds(j * DK, DK)
        normed[at, :] = (attn[at, :] * columns[:, j : j + 1] * gains).astype(BF16)

    def outer(h, carry):
        at = pl.ds(pl.multiple_of(h * DK, DK), DK)
        for r in range(4):
            low, rest = pl.ds(r * DK, DK), ROWS - r * DK
            strip = causal(dot(v[low, at], e[pl.ds(r * DK, rest), at], NT), False)
            dk_part[low, at] = dot(strip, q[pl.ds(r * DK, rest), at], NN)
            dv_part[low, at] = dot(scores_t[h, low, pl.ds(r * DK, rest)], e[pl.ds(r * DK, rest), at], NN)
        return carry

    lax.fori_loop(0, HEADS_HERE, outer, 0)
    start_second(1)

    for mine in (True, False):
        for j in range(2):
            at = half_head(c if mine else 1 - c, j)
            back = halves(state(0, mine, j), 1)
            for r in range(4):
                low = pl.ds(r * DK, DK)
                eh = e[low, at]
                strip = causal(dot(eh, v[pl.ds(0, (r + 1) * DK), at], NT), True)
                total = dot(strip, k[pl.ds(0, (r + 1) * DK), at], NN)
                dq[low, at] = (total + dot(jnp.concatenate([eh, eh], axis=1), back, NT)).astype(BF16)
    start_third(1)
    sib_message(1, 2).wait_recv()
    for mine in (True, False):
        for j in range(2):
            if not mine:
                pref_message(1, j).wait_recv()
            later[half_head(c if mine else 1 - c, j)] = state(1, mine, j)

    for way in range(2):
        for j in range(3):
            sib_message(way, j).wait_send()
        for j in range(2):
            pref_message(way, j).wait_send()
            for phase in range(2):
                for a in range(2):
                    for step in range(1, SIDE):
                        plane_message(way, phase, j, a, step).wait_send()
    for step in range(1, DEPTH):
        zmessage(step).wait_send()


def finish(
    normed, dq, dk_part, dv_part, later, k, v,
    normed_hbm, dq_hbm, dk_hbm, dv_hbm,
    dk, dv, store_sem,
):
    stores = [
        pltpu.make_async_copy(normed, normed_hbm, store_sem.at[0]),
        pltpu.make_async_copy(dq, dq_hbm, store_sem.at[1]),
    ]
    for store in stores:
        store.start()
    for h in range(HEADS_HERE):
        at = head(h)
        back = later[at]
        vh, kh = v[:, at], k[:, at]
        total = dk_part[:, at] + dot(jnp.concatenate([vh, vh], axis=1), halves(back, 1), NT)
        dk[:, at] = total.astype(BF16)
        total = dv_part[:, at] + dot(jnp.concatenate([kh, kh], axis=1), halves(back, 0), NN)
        dv[:, at] = total.astype(BF16)
        for i, (src, dst) in enumerate(((dk, dk_hbm), (dv, dv_hbm))):
            store = pltpu.make_async_copy(src.at[:, at], dst.at[:, at], store_sem.at[2 + 2 * h + i])
            store.start()
            stores.append(store)
    for store in stores:
        store.wait()


def shards(queries, keys, values, gain, d_out):
    width = HEADS_HERE * DK
    block = pltpu.VMEM((ROWS, width), BF16)
    wide = pltpu.VMEM((ROWS, width), F32)
    states = pltpu.VMEM((width, DK), F32)
    in_hbm = pl.BlockSpec(memory_space=pltpu.HBM)
    in_vmem = pl.BlockSpec(memory_space=pltpu.VMEM)
    arguments = (queries, keys, values, gain.reshape(1, width), d_out)
    partial = pl.pallas_call(
        body,
        out_shape=[block, block, wide, wide, states, block, block],
        in_specs=[in_hbm] * 5,
        out_specs=[in_vmem] * 7,
        scratch_shapes=[
            block, block, pltpu.VMEM((1, width), BF16),
            pltpu.VMEM((width, ROWS), BF16),
            pltpu.VMEM((HEADS_HERE, ROWS, ROWS), BF16),
            wide, wide, block,
            pltpu.VMEM((2, width, DK), F32),
            pltpu.VMEM((2, 2, 256, DK), F32),
            pltpu.VMEM((2, 2, 2, 64, DK), F32),
            pltpu.VMEM((2, 2, 2, 3, 64, DK), F32),
            pltpu.VMEM((2, 2, 64, DK), F32),
            pltpu.VMEM((2, 2, 2, 64, DK), F32),
            pltpu.VMEM((2, 2, 2, 3, 64, DK), F32),
            pltpu.VMEM((2, width, DK), F32),
            pltpu.VMEM((8, DK), F32),
            pltpu.VMEM((DEPTH - 1, 8, DK), F32),
            pltpu.SemaphoreType.DMA((5,)),
            pltpu.SemaphoreType.DMA((2, 29)),
            pltpu.SemaphoreType.DMA((2, 29)),
            pltpu.SemaphoreType.DMA((DEPTH - 1,)),
            pltpu.SemaphoreType.DMA((DEPTH - 1,)),
            pltpu.SemaphoreType.REGULAR((3,)),
        ],
        compiler_params=pltpu.CompilerParams(
            collective_id=0, has_side_effects=True, vmem_limit_bytes=32 * 1024 * 1024
        ),
        name="attention",
    )(*[pltpu.with_memory_space_constraint(array, pltpu.HBM) for array in arguments])
    return pl.pallas_call(
        finish,
        out_shape=[jax.ShapeDtypeStruct((ROWS, width), BF16)] * 4,
        in_specs=[in_vmem] * 7,
        out_specs=[in_hbm] * 4,
        scratch_shapes=[block, block, pltpu.SemaphoreType.DMA((10,))],
        compiler_params=pltpu.CompilerParams(vmem_limit_bytes=16 * 1024 * 1024),
        name="finish",
    )(*[pltpu.with_memory_space_constraint(array, pltpu.VMEM) for array in partial])


def solution(mesh):
    in_specs = (P("seq", "head"), P("seq", "head"), P("seq", "head"), P("head"), P("seq", "head"))
    out_specs = (P("seq", "head"), P("seq", "head"), P("seq", "head"), P("seq", "head"))
    return jax.shard_map(shards, mesh=mesh, in_specs=in_specs, out_specs=out_specs, check_vma=False)
```

```python
import functools

import jax
import jax.numpy as jnp
from jax import lax
from jax.experimental import pallas as pl
from jax.experimental.pallas import tpu as pltpu
from jax.sharding import PartitionSpec as P

DK = 128
ROWS = 512
HEADS_HERE = 4
FEATURES = 8192
SIDE = 4
DEPTH = 16
MESH = pl.DeviceIdType.MESH
F32 = jnp.float32
BF16 = jnp.bfloat16

NN = (((1,), (0,)), ((), ()))
NT = (((1,), (1,)), ((), ()))
TN = (((0,), (0,)), ((), ()))


def dot(left, right, dims):
    return lax.dot_general(left, right, dims, preferred_element_type=F32)


def head(h):
    return pl.ds(h * DK, DK)


def halves(state, axis):
    high = state.astype(BF16)
    low = (state - high.astype(F32)).astype(BF16)
    return jnp.concatenate([high, low], axis=axis)


def body(
    q_hbm, k_hbm, v_hbm, gain_hbm, d_hbm,
    normed, dq, dk, dv, dk_part, dv_part, later, k, v,
    q, d, gain,
    qt, scores_t, attn, g, e, inverses, weights,
    own, sib, chip, recv1, row, cols, local, base, recv2, pref,
    zsend, zrecv,
    load_sem, send_sem, recv_sem, zsend_sem, zrecv_sem, near_sem,
):
    s = lax.axis_index("seq")
    z = lax.axis_index("head")
    x, y, c = s // 8, (s // 2) % SIDE, s % 2
    sibling = (s + 1 - 2 * c, z)

    def along_y(step):
        return (x * 8 + ((y + step) % SIDE) * 2 + 1 - c, z)

    def along_x(step):
        return (((x + step) % SIDE) * 8 + y * 2 + 1 - c, z)

    def along_z(step):
        return (s, (z + step) % DEPTH)

    loads = [
        pltpu.make_async_copy(src, dst, load_sem.at[i])
        for i, (src, dst) in enumerate(((k_hbm, k), (v_hbm, v), (q_hbm, q), (d_hbm, d), (gain_hbm, gain)))
    ]
    for load in loads[:2]:
        load.start()

    barrier = pltpu.get_barrier_semaphore()
    partners = [sibling, along_z(1), along_z(DEPTH - 1)]
    partners += [along_y(i) for i in range(1, SIDE)] + [along_x(i) for i in range(1, SIDE)]
    for partner in partners:
        pl.semaphore_signal(barrier, inc=1, device_id=partner, device_id_type=MESH)

    def tell(turn):
        for step in (2**turn, DEPTH - 2**turn):
            pl.semaphore_signal(near_sem.at[turn], inc=1, device_id=along_z(step), device_id_type=MESH)

    def hear(turn):
        pl.semaphore_wait(near_sem.at[turn], 2)

    def half_head(half, j):
        return pl.ds(pl.multiple_of((2 * half + j) * DK, DK), DK)

    def message(way, number, src, dst, device):
        return pltpu.make_async_remote_copy(
            src_ref=src, dst_ref=dst, send_sem=send_sem.at[way, number], recv_sem=recv_sem.at[way, number],
            device_id=device, device_id_type=MESH,
        )

    def sib_message(way, j):
        if j == 2:
            return message(way, 2, own.at[way, pl.ds(256 * c, 256)], sib.at[way, 1], sibling)
        return message(way, j, own.at[way, half_head(1 - c, j)], sib.at[way, 0, pl.ds(j * DK, DK)], sibling)

    def pref_message(way, j):
        return message(way, 3 + j, pref.at[way, half_head(c, j)], pref.at[way, half_head(c, j)], sibling)

    def base_message(way, j):
        return message(way, 5 + j, local.at[way, j], base.at[way, j], sibling)

    def plane_message(way, phase, j, a, step):
        number = 7 + ((phase * 2 + j) * 2 + a) * 3 + step - 1
        device = along_y(step) if phase == a else along_x(step)
        if phase == 0:
            src, dst = chip.at[way, j, a], recv1.at[way, j, a, step - 1]
        elif a == 0:
            src, dst = row.at[way, j], recv2.at[way, j, a, step - 1]
        else:
            wrapped = (y + step) // SIDE
            pick = 1 - wrapped if way == 0 else wrapped
            src, dst = cols.at[way, j, pick], recv2.at[way, j, a, step - 1]
        return message(way, number, src, dst, device)

    def zmessage(step):
        return pltpu.make_async_remote_copy(
            src_ref=zsend, dst_ref=zrecv.at[step - 1], send_sem=zsend_sem.at[step - 1],
            recv_sem=zrecv_sem.at[step - 1], device_id=along_z(step), device_id_type=MESH,
        )

    def counts(way, step, place):
        return step <= place if way == 0 else step > place

    def start_first(way):
        for j in range(2):
            sib_message(way, j).wait_recv()
            total = own[way, half_head(c, j)] + sib[way, 0, pl.ds(j * DK, DK)]
            for a in range(2):
                chip[way, j, a] = total[64 * a : 64 * a + 64]
            for step in (2, 1, 3):
                for a in range(2):
                    plane_message(way, 0, j, a, step).start()

    def start_second(way):
        for j in range(2):
            for a in range(2):
                for step in range(1, SIDE):
                    plane_message(way, 0, j, a, step).wait_recv()
                if j + a == 0:
                    sib_message(way, 2).wait_recv()
                mine = own[way, pl.ds(256 * (1 - c) + j * DK + 64 * a, 64)] + sib[way, 1, pl.ds(j * DK + 64 * a, 64)]
                if a == 0:
                    total, before = mine, jnp.zeros_like(mine)
                    for step in range(1, SIDE):
                        block = recv1[way, j, a, step - 1]
                        total = total + block
                        before = before + jnp.where(counts(way, step, y), block, 0.0)
                    row[way, j] = total
                    local[way, j, pl.ds(0, 64)] = before
                else:
                    column = jnp.zeros_like(mine)
                    for step in range(1, SIDE):
                        column = column + jnp.where(counts(way, step, x), recv1[way, j, a, step - 1], 0.0)
                    cols[way, j, 0] = column
                    local[way, j, pl.ds(64, 64)] = column
                    cols[way, j, 1] = column + mine
                for step in (2, 1, 3):
                    plane_message(way, 1, j, a, step).start()
            base_message(way, j).start()

    def start_third(way):
        for j in range(2):
            base_message(way, j).wait_recv()
            for a in range(2):
                for step in range(1, SIDE):
                    plane_message(way, 1, j, a, step).wait_recv()
                total = base[way, j, pl.ds(64 * a, 64)]
                for step in range(1, SIDE):
                    block = recv2[way, j, a, step - 1]
                    total = total + (jnp.where(counts(way, step, x), block, 0.0) if a == 0 else block)
                pref[way, pl.ds(256 * c + j * DK + 64 * a, 64)] = total
            pref_message(way, j).start()

    def state(way, mine, j):
        add = c == 1 if way == 0 else c == 0
        block = sib[way, 0 if mine else 1, pl.ds(j * DK, DK)]
        return pref[way, half_head(c if mine else 1 - c, j)] + jnp.where(add, block, 0.0)

    steps0 = lax.broadcasted_iota(jnp.int32, (DK, DK), 0)
    steps1 = lax.broadcasted_iota(jnp.int32, (DK, DK), 1)

    def causal(block, lower):
        keep = steps0 >= steps1 if lower else steps0 <= steps1
        if block.shape[1] == DK:
            return jnp.where(keep, block, 0.0).astype(BF16)
        if lower:
            cut = block.shape[1] - DK
            return jnp.concatenate(
                [block[:, :cut].astype(BF16), jnp.where(keep, block[:, cut:], 0.0).astype(BF16)], axis=1
            )
        return jnp.concatenate(
            [jnp.where(keep, block[:, :DK], 0.0).astype(BF16), block[:, DK:].astype(BF16)], axis=1
        )

    loads[0].wait()
    loads[1].wait()
    for load in loads[2:]:
        load.start()
    for j in range(2):
        at = half_head(1 - c, j)
        own[0, at] = dot(k[:, at], v[:, at], TN)
    pl.semaphore_wait(barrier, len(partners))
    tell(0)
    for j in range(2):
        sib_message(0, j).start()
    for j in range(2):
        at = half_head(c, j)
        own[0, at] = dot(k[:, at], v[:, at], TN)
    sib_message(0, 2).start()
    loads[2].wait()
    loads[3].wait()
    loads[4].wait()
    start_first(0)

    def inner(h, carry):
        at = pl.ds(pl.multiple_of(h * DK, DK), DK)
        for r in range(4):
            strip = causal(dot(q[pl.ds(r * DK, DK), at], k[pl.ds(0, (r + 1) * DK), at], NT), True)
            attn[pl.ds(r * DK, DK), at] = dot(strip, v[pl.ds(0, (r + 1) * DK), at], NN)
        return carry

    lax.fori_loop(0, HEADS_HERE, inner, 0)
    hear(0)
    tell(1)
    start_second(0)

    def prepare(h, carry):
        at = pl.ds(pl.multiple_of(h * DK, DK), DK)
        qt[at, :] = q[:, at].astype(F32).T.astype(BF16)
        for r in range(4):
            rest = ROWS - r * DK
            strip = dot(k[pl.ds(r * DK, DK), at], q[pl.ds(r * DK, rest), at], NT)
            scores_t[h, pl.ds(r * DK, DK), pl.ds(r * DK, rest)] = causal(strip, False)
        return carry

    lax.fori_loop(0, HEADS_HERE, prepare, 0)
    for h in range(HEADS_HERE):
        g[:, head(h)] = d[:, head(h)].astype(F32) * gain[h : h + 1, :].astype(F32)
    hear(1)
    tell(2)
    start_third(0)

    squares = jnp.zeros((ROWS, DK), F32)
    products = jnp.zeros((ROWS, DK), F32)
    for mine in (True, False):
        for j in range(2):
            if not mine:
                pref_message(0, j).wait_recv()
            at = half_head(c if mine else 1 - c, j)
            qh = q[:, at]
            total = attn[:, at] + dot(jnp.concatenate([qh, qh], axis=1), halves(state(0, mine, j), 0), NN)
            attn[:, at] = total
            squares = squares + total * total
            products = products + total * g[:, at]

    ones = jnp.ones((8, 3 * DK), BF16)

    def row_sums(array):
        high = array.astype(BF16)
        rest = array - high.astype(F32)
        middle = rest.astype(BF16)
        low = (rest - middle.astype(F32)).astype(BF16)
        return dot(ones, jnp.concatenate([high, middle, low], axis=1), NT)

    for i, array in enumerate((squares, products)):
        sums = row_sums(array)
        for j in range(4):
            zsend[pl.ds(4 * i + j, 1), :] = sums[0:1, j * DK : (j + 1) * DK]
    hear(2)
    for step in (8, 7, 9, 6, 10, 5, 11, 4, 12, 3, 13, 2, 14, 1, 15):
        zmessage(step).start()

    totals = zsend[...]
    for step in (1, 15, 2, 14, 3, 13, 4, 12, 5, 11, 6, 10, 7, 9, 8):
        zmessage(step).wait_recv()
        totals = totals + zrecv[step - 1]
    means = totals / FEATURES
    rms = jnp.sqrt(means[0:4] + 1e-05)
    inverse = 1.0 / rms
    weight = means[4:8] * inverse * inverse
    columns = jnp.concatenate([inverse, weight], axis=0).T
    for j in range(4):
        inverses[pl.ds(j * DK, DK), :] = jnp.broadcast_to(columns[:, j : j + 1], (DK, DK))
        weights[pl.ds(j * DK, DK), :] = jnp.broadcast_to(columns[:, 4 + j : 5 + j], (DK, DK))
    for mine in (False, True):
        for j in range(2):
            at = half_head(c if mine else 1 - c, j)
            delta = ((g[:, at] - attn[:, at] * weights[...]) * inverses[...]).astype(BF16)
            e[:, at] = delta
            own[1, at] = dot(qt[at, :], delta, NN)
            if not mine:
                sib_message(1, j).start()
    sib_message(1, 2).start()
    start_first(1)
    for h in range(HEADS_HERE):
        normed[:, head(h)] = (attn[:, head(h)] * inverses[...] * gain[h : h + 1, :].astype(F32)).astype(BF16)

    def outer(h, carry):
        at = pl.ds(pl.multiple_of(h * DK, DK), DK)
        for r in range(4):
            low, rest = pl.ds(r * DK, DK), ROWS - r * DK
            strip = causal(dot(v[low, at], e[pl.ds(r * DK, rest), at], NT), False)
            dk_part[low, at] = dot(strip, q[pl.ds(r * DK, rest), at], NN)
            dv_part[low, at] = dot(scores_t[h, low, pl.ds(r * DK, rest)], e[pl.ds(r * DK, rest), at], NN)
        return carry

    lax.fori_loop(0, HEADS_HERE, outer, 0)
    start_second(1)

    for mine in (True, False):
        for j in range(2):
            at = half_head(c if mine else 1 - c, j)
            back = halves(state(0, mine, j), 1)
            for r in range(4):
                low = pl.ds(r * DK, DK)
                eh = e[low, at]
                strip = causal(dot(eh, v[pl.ds(0, (r + 1) * DK), at], NT), True)
                total = dot(strip, k[pl.ds(0, (r + 1) * DK), at], NN)
                dq[low, at] = (total + dot(jnp.concatenate([eh, eh], axis=1), back, NT)).astype(BF16)
    start_third(1)
    for mine in (True, False):
        for j in range(2):
            at = half_head(c if mine else 1 - c, j)
            if mine:
                last_products(at, state(1, mine, j), k, v, dk_part, dv_part, dk, dv)
            else:
                pref_message(1, j).wait_recv()
                later[pl.ds(j * DK, DK)] = state(1, mine, j)

    for way in range(2):
        for j in range(3):
            sib_message(way, j).wait_send()
        for j in range(2):
            pref_message(way, j).wait_send()
            base_message(way, j).wait_send()
            for phase in range(2):
                for a in range(2):
                    for step in range(1, SIDE):
                        plane_message(way, phase, j, a, step).wait_send()
    for step in range(1, DEPTH):
        zmessage(step).wait_send()


def last_products(at, back, k, v, dk_part, dv_part, dk, dv):
    vh, kh = v[:, at], k[:, at]
    total = dk_part[:, at] + dot(jnp.concatenate([vh, vh], axis=1), halves(back, 1), NT)
    dk[:, at] = total.astype(BF16)
    total = dv_part[:, at] + dot(jnp.concatenate([kh, kh], axis=1), halves(back, 0), NN)
    dv[:, at] = total.astype(BF16)


def finish(
    normed, dq, dk_mine, dv_mine, dk_part, dv_part, later, k, v,
    normed_hbm, dq_hbm, dk_hbm, dv_hbm,
    dk, dv, store_sem,
):
    c = lax.axis_index("seq") % 2
    stores = []

    def store(src, dst):
        copy = pltpu.make_async_copy(src, dst, store_sem.at[len(stores)])
        copy.start()
        stores.append(copy)

    here = pl.ds(pl.multiple_of(256 * c, 256), 256)
    store(dk_mine.at[:, here], dk_hbm.at[:, here])
    store(dv_mine.at[:, here], dv_hbm.at[:, here])
    for part in range(2):
        rows = pl.ds(256 * part, 256)
        store(normed.at[rows], normed_hbm.at[rows])
        store(dq.at[rows], dq_hbm.at[rows])
    for j in range(2):
        at = pl.ds(pl.multiple_of((2 * (1 - c) + j) * DK, DK), DK)
        last_products(at, later[pl.ds(j * DK, DK)], k, v, dk_part, dv_part, dk, dv)
        store(dk.at[:, at], dk_hbm.at[:, at])
        store(dv.at[:, at], dv_hbm.at[:, at])
    for copy in stores:
        copy.wait()


def shards(queries, keys, values, gain, d_out):
    width = HEADS_HERE * DK
    block = pltpu.VMEM((ROWS, width), BF16)
    wide = pltpu.VMEM((ROWS, width), F32)
    states = pltpu.VMEM((256, DK), F32)
    in_hbm = pl.BlockSpec(memory_space=pltpu.HBM)
    in_vmem = pl.BlockSpec(memory_space=pltpu.VMEM)
    arguments = (queries, keys, values, gain.reshape(HEADS_HERE, DK), d_out)
    partial = pl.pallas_call(
        body,
        out_shape=[block, block, block, block, wide, wide, states, block, block],
        in_specs=[in_hbm] * 5,
        out_specs=[in_vmem] * 9,
        scratch_shapes=[
            block, block, pltpu.VMEM((HEADS_HERE, DK), BF16),
            pltpu.VMEM((width, ROWS), BF16),
            pltpu.VMEM((HEADS_HERE, ROWS, ROWS), BF16),
            wide, wide, block, pltpu.VMEM((ROWS, DK), F32), pltpu.VMEM((ROWS, DK), F32),
            pltpu.VMEM((2, width, DK), F32),
            pltpu.VMEM((2, 2, 256, DK), F32),
            pltpu.VMEM((2, 2, 2, 64, DK), F32),
            pltpu.VMEM((2, 2, 2, 3, 64, DK), F32),
            pltpu.VMEM((2, 2, 64, DK), F32),
            pltpu.VMEM((2, 2, 2, 64, DK), F32),
            pltpu.VMEM((2, 2, DK, DK), F32),
            pltpu.VMEM((2, 2, DK, DK), F32),
            pltpu.VMEM((2, 2, 2, 3, 64, DK), F32),
            pltpu.VMEM((2, width, DK), F32),
            pltpu.VMEM((8, DK), F32),
            pltpu.VMEM((DEPTH - 1, 8, DK), F32),
            pltpu.SemaphoreType.DMA((5,)),
            pltpu.SemaphoreType.DMA((2, 31)),
            pltpu.SemaphoreType.DMA((2, 31)),
            pltpu.SemaphoreType.DMA((DEPTH - 1,)),
            pltpu.SemaphoreType.DMA((DEPTH - 1,)),
            pltpu.SemaphoreType.REGULAR((3,)),
        ],
        compiler_params=pltpu.CompilerParams(
            collective_id=0, has_side_effects=True, vmem_limit_bytes=32 * 1024 * 1024
        ),
        name="attention",
    )(*[pltpu.with_memory_space_constraint(array, pltpu.HBM) for array in arguments])
    return pl.pallas_call(
        finish,
        out_shape=[jax.ShapeDtypeStruct((ROWS, width), BF16)] * 4,
        in_specs=[in_vmem] * 9,
        out_specs=[in_hbm] * 4,
        scratch_shapes=[block, block, pltpu.SemaphoreType.DMA((10,))],
        compiler_params=pltpu.CompilerParams(vmem_limit_bytes=16 * 1024 * 1024),
        name="finish",
    )(*[pltpu.with_memory_space_constraint(array, pltpu.VMEM) for array in partial])


def solution(mesh):
    in_specs = (P("seq", "head"), P("seq", "head"), P("seq", "head"), P("head"), P("seq", "head"))
    out_specs = (P("seq", "head"), P("seq", "head"), P("seq", "head"), P("seq", "head"))
    return jax.shard_map(shards, mesh=mesh, in_specs=in_specs, out_specs=out_specs, check_vma=False)
```

```python
import functools

import jax
import jax.numpy as jnp
from jax import lax
from jax.experimental import pallas as pl
from jax.experimental.pallas import tpu as pltpu
from jax.sharding import PartitionSpec as P

DK = 128
ROWS = 512
HEADS_HERE = 4
FEATURES = 8192
SIDE = 4
DEPTH = 16
MESH = pl.DeviceIdType.MESH
F32 = jnp.float32
BF16 = jnp.bfloat16

NN = (((1,), (0,)), ((), ()))
NT = (((1,), (1,)), ((), ()))
TN = (((0,), (0,)), ((), ()))


def dot(left, right, dims):
    return lax.dot_general(left, right, dims, preferred_element_type=F32)


def head(h):
    return pl.ds(h * DK, DK)


def halves(state, axis):
    high = state.astype(BF16)
    low = (state - high.astype(F32)).astype(BF16)
    return jnp.concatenate([high, low], axis=axis)


def body(
    q_hbm, k_hbm, v_hbm, gain_hbm, d_hbm,
    normed, dq, dk, dv, dk_part, dv_part, later, k, v,
    q, d, gain,
    qt, scores_t, attn, g, e, inverses, weights,
    own, sib, chip, recv1, row, cols, local, base, recv2, pref,
    zsend, zrecv,
    load_sem, send_sem, recv_sem, zsend_sem, zrecv_sem, near_sem,
):
    s = lax.axis_index("seq")
    z = lax.axis_index("head")
    x, y, c = s // 8, (s // 2) % SIDE, s % 2
    sibling = (s + 1 - 2 * c, z)

    def along_y(step):
        return (x * 8 + ((y + step) % SIDE) * 2 + 1 - c, z)

    def along_x(step):
        return (((x + step) % SIDE) * 8 + y * 2 + 1 - c, z)

    def along_z(step):
        return (s, (z + step) % DEPTH)

    here, there = pl.ds(pl.multiple_of(256 * c, 256), 256), pl.ds(pl.multiple_of(256 - 256 * c, 256), 256)
    loads = [
        pltpu.make_async_copy(src, dst, load_sem.at[i])
        for i, (src, dst) in enumerate(
            (
                (k_hbm.at[:, there], k.at[:, there]),
                (v_hbm.at[:, there], v.at[:, there]),
                (k_hbm.at[:, here], k.at[:, here]),
                (v_hbm.at[:, here], v.at[:, here]),
                (q_hbm, q),
                (d_hbm, d),
                (gain_hbm, gain),
            )
        )
    ]
    for load in loads[:4]:
        load.start()

    barrier = pltpu.get_barrier_semaphore()
    partners = [sibling, along_z(1), along_z(DEPTH - 1)]
    partners += [along_y(i) for i in range(1, SIDE)] + [along_x(i) for i in range(1, SIDE)]
    for partner in partners:
        pl.semaphore_signal(barrier, inc=1, device_id=partner, device_id_type=MESH)

    def tell(turn):
        for step in (2**turn, DEPTH - 2**turn):
            pl.semaphore_signal(near_sem.at[turn], inc=1, device_id=along_z(step), device_id_type=MESH)

    def hear(turn):
        pl.semaphore_wait(near_sem.at[turn], 2)

    def half_head(half, j):
        return pl.ds(pl.multiple_of((2 * half + j) * DK, DK), DK)

    def message(way, number, src, dst, device):
        return pltpu.make_async_remote_copy(
            src_ref=src, dst_ref=dst, send_sem=send_sem.at[way, number], recv_sem=recv_sem.at[way, number],
            device_id=device, device_id_type=MESH,
        )

    def sib_message(way, j):
        if j == 2:
            return message(way, 2, own.at[way, pl.ds(256 * c, 256)], sib.at[way, 1], sibling)
        return message(way, j, own.at[way, half_head(1 - c, j)], sib.at[way, 0, pl.ds(j * DK, DK)], sibling)

    def pref_message(way, j):
        return message(way, 3 + j, pref.at[way, half_head(c, j)], pref.at[way, half_head(c, j)], sibling)

    def base_message(way, j):
        return message(way, 5 + j, local.at[way, j], base.at[way, j], sibling)

    def plane_message(way, phase, j, a, step):
        number = 7 + ((phase * 2 + j) * 2 + a) * 3 + step - 1
        device = along_y(step) if phase == a else along_x(step)
        if phase == 0:
            src, dst = chip.at[way, j, a], recv1.at[way, j, a, step - 1]
        elif a == 0:
            src, dst = row.at[way, j], recv2.at[way, j, a, step - 1]
        else:
            wrapped = (y + step) // SIDE
            pick = 1 - wrapped if way == 0 else wrapped
            src, dst = cols.at[way, j, pick], recv2.at[way, j, a, step - 1]
        return message(way, number, src, dst, device)

    def zmessage(step):
        return pltpu.make_async_remote_copy(
            src_ref=zsend, dst_ref=zrecv.at[step - 1], send_sem=zsend_sem.at[step - 1],
            recv_sem=zrecv_sem.at[step - 1], device_id=along_z(step), device_id_type=MESH,
        )

    def counts(way, step, place):
        return step <= place if way == 0 else step > place

    def start_plane(way, phase, j, a):
        for step in (2, 1, 3):
            if phase == a:
                plane_message(way, phase, j, a, step).start()
            else:
                pl.when(reaches(way, step))(plane_message(way, phase, j, a, step).start)

    def wait_plane(way, phase, j, a):
        for step in range(1, SIDE):
            if phase == a:
                plane_message(way, phase, j, a, step).wait_recv()
            else:
                pl.when(counts(way, step, x))(plane_message(way, phase, j, a, step).wait_recv)

    def leave_plane(way, phase, j, a):
        for step in range(1, SIDE):
            if phase == a:
                plane_message(way, phase, j, a, step).wait_send()
            else:
                pl.when(reaches(way, step))(plane_message(way, phase, j, a, step).wait_send)

    def reaches(way, step):
        return x + step < SIDE if way == 0 else x + step >= SIDE

    def start_first(way):
        for j in range(2):
            sib_message(way, j).wait_recv()
            total = own[way, half_head(c, j)] + sib[way, 0, pl.ds(j * DK, DK)]
            for a in range(2):
                chip[way, j, a] = total[64 * a : 64 * a + 64]
            for a in range(2):
                start_plane(way, 0, j, a)

    def start_second(way):
        sib_message(way, 2).wait_recv()
        for a in (1, 0):
            for j in range(2):
                wait_plane(way, 0, j, a)
                rows = pl.ds(j * DK + 64 * a, 64)
                mine = own[way, pl.ds(256 * (1 - c) + j * DK + 64 * a, 64)] + sib[way, 1, rows]
                if a == 0:
                    total, before = mine, jnp.zeros_like(mine)
                    for step in range(1, SIDE):
                        block = recv1[way, j, a, step - 1]
                        total = total + block
                        before = before + jnp.where(counts(way, step, y), block, 0.0)
                    row[way, j] = total
                    local[way, j, pl.ds(0, 64)] = before
                else:
                    column = jnp.zeros_like(mine)
                    for step in range(1, SIDE):
                        column = column + jnp.where(counts(way, step, x), recv1[way, j, a, step - 1], 0.0)
                    cols[way, j, 0] = column
                    cols[way, j, 1] = column + mine
                    local[way, j, pl.ds(64, 64)] = column
                start_plane(way, 1, j, a)
                if a == 0:
                    base_message(way, j).start()

    def start_third(way):
        for j in range(2):
            base_message(way, j).wait_recv()
            for a in range(2):
                wait_plane(way, 1, j, a)
                total = base[way, j, pl.ds(64 * a, 64)]
                for step in range(1, SIDE):
                    block = recv2[way, j, a, step - 1]
                    total = total + (jnp.where(counts(way, step, x), block, 0.0) if a == 0 else block)
                pref[way, pl.ds(256 * c + j * DK + 64 * a, 64)] = total
            pref_message(way, j).start()

    def state(way, mine, j):
        add = c == 1 if way == 0 else c == 0
        block = sib[way, 0 if mine else 1, pl.ds(j * DK, DK)]
        return pref[way, half_head(c if mine else 1 - c, j)] + jnp.where(add, block, 0.0)

    steps0 = lax.broadcasted_iota(jnp.int32, (DK, DK), 0)
    steps1 = lax.broadcasted_iota(jnp.int32, (DK, DK), 1)

    def causal(block, lower):
        keep = steps0 >= steps1 if lower else steps0 <= steps1
        if block.shape[1] == DK:
            return jnp.where(keep, block, 0.0).astype(BF16)
        if lower:
            cut = block.shape[1] - DK
            return jnp.concatenate(
                [block[:, :cut].astype(BF16), jnp.where(keep, block[:, cut:], 0.0).astype(BF16)], axis=1
            )
        return jnp.concatenate(
            [jnp.where(keep, block[:, :DK], 0.0).astype(BF16), block[:, DK:].astype(BF16)], axis=1
        )

    for load in loads[:2]:
        load.wait()
    for load in loads[4:]:
        load.start()
    for j in range(2):
        at = half_head(1 - c, j)
        own[0, at] = dot(k[:, at], v[:, at], TN)
    pl.semaphore_wait(barrier, len(partners))
    tell(0)
    for j in range(2):
        sib_message(0, j).start()
    for load in loads[2:4]:
        load.wait()
    for j in range(2):
        at = half_head(c, j)
        own[0, at] = dot(k[:, at], v[:, at], TN)
    sib_message(0, 2).start()
    for load in loads[4:]:
        load.wait()
    start_first(0)

    def inner(h, carry):
        at = pl.ds(pl.multiple_of(h * DK, DK), DK)
        for r in range(4):
            strip = causal(dot(q[pl.ds(r * DK, DK), at], k[pl.ds(0, (r + 1) * DK), at], NT), True)
            attn[pl.ds(r * DK, DK), at] = dot(strip, v[pl.ds(0, (r + 1) * DK), at], NN)
        return carry

    lax.fori_loop(0, HEADS_HERE, inner, 0)
    hear(0)
    tell(1)
    start_second(0)

    def prepare(h, carry):
        at = pl.ds(pl.multiple_of(h * DK, DK), DK)
        qt[at, :] = q[:, at].astype(F32).T.astype(BF16)
        for r in range(4):
            rest = ROWS - r * DK
            strip = dot(k[pl.ds(r * DK, DK), at], q[pl.ds(r * DK, rest), at], NT)
            scores_t[h, pl.ds(r * DK, DK), pl.ds(r * DK, rest)] = causal(strip, False)
        return carry

    lax.fori_loop(0, HEADS_HERE, prepare, 0)
    for h in range(HEADS_HERE):
        g[:, head(h)] = d[:, head(h)].astype(F32) * gain[h : h + 1, :].astype(F32)
    hear(1)
    tell(2)
    start_third(0)

    squares = jnp.zeros((ROWS, DK), F32)
    products = jnp.zeros((ROWS, DK), F32)
    for mine in (True, False):
        for j in range(2):
            if not mine:
                pref_message(0, j).wait_recv()
            at = half_head(c if mine else 1 - c, j)
            qh = q[:, at]
            total = attn[:, at] + dot(jnp.concatenate([qh, qh], axis=1), halves(state(0, mine, j), 0), NN)
            attn[:, at] = total
            squares = squares + total * total
            products = products + total * g[:, at]

    ones = jnp.ones((8, 3 * DK), BF16)

    def row_sums(array):
        high = array.astype(BF16)
        rest = array - high.astype(F32)
        middle = rest.astype(BF16)
        low = (rest - middle.astype(F32)).astype(BF16)
        return dot(ones, jnp.concatenate([high, middle, low], axis=1), NT)

    for i, array in enumerate((squares, products)):
        sums = row_sums(array)
        for j in range(4):
            zsend[pl.ds(4 * i + j, 1), :] = sums[0:1, j * DK : (j + 1) * DK]
    hear(2)
    for step in (8, 7, 9, 6, 10, 5, 11, 4, 12, 3, 13, 2, 14, 1, 15):
        zmessage(step).start()

    totals = zsend[...]
    for step in (1, 15, 2, 14, 3, 13, 4, 12, 5, 11, 6, 10, 7, 9, 8):
        zmessage(step).wait_recv()
        totals = totals + zrecv[step - 1]
    means = totals / FEATURES
    rms = jnp.sqrt(means[0:4] + 1e-05)
    inverse = 1.0 / rms
    weight = means[4:8] * inverse * inverse
    columns = jnp.concatenate([inverse, weight], axis=0).T
    for j in range(4):
        inverses[pl.ds(j * DK, DK), :] = jnp.broadcast_to(columns[:, j : j + 1], (DK, DK))
        weights[pl.ds(j * DK, DK), :] = jnp.broadcast_to(columns[:, 4 + j : 5 + j], (DK, DK))
    for mine in (False, True):
        for j in range(2):
            at = half_head(c if mine else 1 - c, j)
            delta = ((g[:, at] - attn[:, at] * weights[...]) * inverses[...]).astype(BF16)
            e[:, at] = delta
            own[1, at] = dot(qt[at, :], delta, NN)
            if not mine:
                sib_message(1, j).start()
    sib_message(1, 2).start()
    start_first(1)
    for h in range(HEADS_HERE):
        normed[:, head(h)] = (attn[:, head(h)] * inverses[...] * gain[h : h + 1, :].astype(F32)).astype(BF16)

    def outer(h, carry):
        at = pl.ds(pl.multiple_of(h * DK, DK), DK)
        for r in range(4):
            low, rest = pl.ds(r * DK, DK), ROWS - r * DK
            strip = causal(dot(v[low, at], e[pl.ds(r * DK, rest), at], NT), False)
            dk_part[low, at] = dot(strip, q[pl.ds(r * DK, rest), at], NN)
            dv_part[low, at] = dot(scores_t[h, low, pl.ds(r * DK, rest)], e[pl.ds(r * DK, rest), at], NN)
        return carry

    lax.fori_loop(0, HEADS_HERE, outer, 0)
    start_second(1)

    for mine in (True, False):
        for j in range(2):
            at = half_head(c if mine else 1 - c, j)
            back = halves(state(0, mine, j), 1)
            for r in range(4):
                low = pl.ds(r * DK, DK)
                eh = e[low, at]
                strip = causal(dot(eh, v[pl.ds(0, (r + 1) * DK), at], NT), True)
                total = dot(strip, k[pl.ds(0, (r + 1) * DK), at], NN)
                dq[low, at] = (total + dot(jnp.concatenate([eh, eh], axis=1), back, NT)).astype(BF16)
    start_third(1)
    for mine in (True, False):
        for j in range(2):
            at = half_head(c if mine else 1 - c, j)
            if mine:
                last_products(at, state(1, mine, j), k, v, dk_part, dv_part, dk, dv)
            else:
                pref_message(1, j).wait_recv()
                later[pl.ds(j * DK, DK)] = state(1, mine, j)

    for way in range(2):
        for j in range(3):
            sib_message(way, j).wait_send()
        for j in range(2):
            pref_message(way, j).wait_send()
            base_message(way, j).wait_send()
            for phase in range(2):
                for a in range(2):
                    leave_plane(way, phase, j, a)
    for step in range(1, DEPTH):
        zmessage(step).wait_send()


def last_products(at, back, k, v, dk_part, dv_part, dk, dv):
    vh, kh = v[:, at], k[:, at]
    total = dk_part[:, at] + dot(jnp.concatenate([vh, vh], axis=1), halves(back, 1), NT)
    dk[:, at] = total.astype(BF16)
    total = dv_part[:, at] + dot(jnp.concatenate([kh, kh], axis=1), halves(back, 0), NN)
    dv[:, at] = total.astype(BF16)


def finish(
    normed, dq, dk_mine, dv_mine, dk_part, dv_part, later, k, v,
    normed_hbm, dq_hbm, dk_hbm, dv_hbm,
    dk, dv, store_sem,
):
    c = lax.axis_index("seq") % 2
    stores = []

    def store(src, dst):
        copy = pltpu.make_async_copy(src, dst, store_sem.at[len(stores)])
        copy.start()
        stores.append(copy)

    here = pl.ds(pl.multiple_of(256 * c, 256), 256)
    store(dk_mine.at[:, here], dk_hbm.at[:, here])
    store(dv_mine.at[:, here], dv_hbm.at[:, here])
    for part in range(2):
        rows = pl.ds(256 * part, 256)
        store(normed.at[rows], normed_hbm.at[rows])
        store(dq.at[rows], dq_hbm.at[rows])
    for j in range(2):
        at = pl.ds(pl.multiple_of((2 * (1 - c) + j) * DK, DK), DK)
        last_products(at, later[pl.ds(j * DK, DK)], k, v, dk_part, dv_part, dk, dv)
        store(dk.at[:, at], dk_hbm.at[:, at])
        store(dv.at[:, at], dv_hbm.at[:, at])
    for copy in stores:
        copy.wait()


def shards(queries, keys, values, gain, d_out):
    width = HEADS_HERE * DK
    block = pltpu.VMEM((ROWS, width), BF16)
    wide = pltpu.VMEM((ROWS, width), F32)
    states = pltpu.VMEM((256, DK), F32)
    in_hbm = pl.BlockSpec(memory_space=pltpu.HBM)
    in_vmem = pl.BlockSpec(memory_space=pltpu.VMEM)
    arguments = (queries, keys, values, gain.reshape(HEADS_HERE, DK), d_out)
    partial = pl.pallas_call(
        body,
        out_shape=[block, block, block, block, wide, wide, states, block, block],
        in_specs=[in_hbm] * 5,
        out_specs=[in_vmem] * 9,
        scratch_shapes=[
            block, block, pltpu.VMEM((HEADS_HERE, DK), BF16),
            pltpu.VMEM((width, ROWS), BF16),
            pltpu.VMEM((HEADS_HERE, ROWS, ROWS), BF16),
            wide, wide, block, pltpu.VMEM((ROWS, DK), F32), pltpu.VMEM((ROWS, DK), F32),
            pltpu.VMEM((2, width, DK), F32),
            pltpu.VMEM((2, 2, 256, DK), F32),
            pltpu.VMEM((2, 2, 2, 64, DK), F32),
            pltpu.VMEM((2, 2, 2, 3, 64, DK), F32),
            pltpu.VMEM((2, 2, 64, DK), F32),
            pltpu.VMEM((2, 2, 2, 64, DK), F32),
            pltpu.VMEM((2, 2, DK, DK), F32),
            pltpu.VMEM((2, 2, DK, DK), F32),
            pltpu.VMEM((2, 2, 2, 3, 64, DK), F32),
            pltpu.VMEM((2, width, DK), F32),
            pltpu.VMEM((8, DK), F32),
            pltpu.VMEM((DEPTH - 1, 8, DK), F32),
            pltpu.SemaphoreType.DMA((7,)),
            pltpu.SemaphoreType.DMA((2, 31)),
            pltpu.SemaphoreType.DMA((2, 31)),
            pltpu.SemaphoreType.DMA((DEPTH - 1,)),
            pltpu.SemaphoreType.DMA((DEPTH - 1,)),
            pltpu.SemaphoreType.REGULAR((3,)),
        ],
        compiler_params=pltpu.CompilerParams(
            collective_id=0, has_side_effects=True, vmem_limit_bytes=32 * 1024 * 1024
        ),
        name="attention",
    )(*[pltpu.with_memory_space_constraint(array, pltpu.HBM) for array in arguments])
    return pl.pallas_call(
        finish,
        out_shape=[jax.ShapeDtypeStruct((ROWS, width), BF16)] * 4,
        in_specs=[in_vmem] * 9,
        out_specs=[in_hbm] * 4,
        scratch_shapes=[block, block, pltpu.SemaphoreType.DMA((10,))],
        compiler_params=pltpu.CompilerParams(vmem_limit_bytes=16 * 1024 * 1024),
        name="finish",
    )(*[pltpu.with_memory_space_constraint(array, pltpu.VMEM) for array in partial])


def solution(mesh):
    in_specs = (P("seq", "head"), P("seq", "head"), P("seq", "head"), P("head"), P("seq", "head"))
    out_specs = (P("seq", "head"), P("seq", "head"), P("seq", "head"), P("seq", "head"))
    return jax.shard_map(shards, mesh=mesh, in_specs=in_specs, out_specs=out_specs, check_vma=False)
```

```python
import functools

import jax
import jax.numpy as jnp
from jax import lax
from jax.experimental import pallas as pl
from jax.experimental.pallas import tpu as pltpu
from jax.sharding import PartitionSpec as P

DK = 128
ROWS = 512
HEADS_HERE = 4
PIECES = 4
PIECE = 256 // PIECES
PART = PIECE // 2
FEATURES = 8192
SIDE = 4
DEPTH = 16
MESH = pl.DeviceIdType.MESH
F32 = jnp.float32
BF16 = jnp.bfloat16

NN = (((1,), (0,)), ((), ()))
NT = (((1,), (1,)), ((), ()))
TN = (((0,), (0,)), ((), ()))


def dot(left, right, dims):
    return lax.dot_general(left, right, dims, preferred_element_type=F32)


def head(h):
    return pl.ds(h * DK, DK)


def halves(state, axis):
    high = state.astype(BF16)
    low = (state - high.astype(F32)).astype(BF16)
    return jnp.concatenate([high, low], axis=axis)


def body(
    q_hbm, k_hbm, v_hbm, gain_hbm, d_hbm,
    normed, dq, dk, dv, dk_part, dv_part, later, k, v,
    q, d, gain,
    qt, scores_t, attn, g, e, inverses, weights,
    own, sib, chip, recv1, row, cols, local, base, recv2, pref,
    zsend, zrecv,
    load_sem, send_sem, sib_sem, pref_sem, base_sem, plane_sem, zsend_sem, zrecv_sem, near_sem,
):
    s = lax.axis_index("seq")
    z = lax.axis_index("head")
    x, y, c = s // 8, (s // 2) % SIDE, s % 2
    sibling = (s + 1 - 2 * c, z)

    def along_y(step):
        return (x * 8 + ((y + step) % SIDE) * 2 + 1 - c, z)

    def along_x(step):
        return (((x + step) % SIDE) * 8 + y * 2 + 1 - c, z)

    def along_z(step):
        return (s, (z + step) % DEPTH)

    here, there = pl.ds(pl.multiple_of(256 * c, 256), 256), pl.ds(pl.multiple_of(256 - 256 * c, 256), 256)
    loads = [
        pltpu.make_async_copy(src, dst, load_sem.at[i])
        for i, (src, dst) in enumerate(
            (
                (k_hbm.at[:, there], k.at[:, there]),
                (v_hbm.at[:, there], v.at[:, there]),
                (k_hbm.at[:, here], k.at[:, here]),
                (v_hbm.at[:, here], v.at[:, here]),
                (q_hbm, q),
                (d_hbm, d),
                (gain_hbm, gain),
            )
        )
    ]
    for load in loads[:4]:
        load.start()

    barrier = pltpu.get_barrier_semaphore()
    partners = [sibling, along_z(1), along_z(DEPTH - 1)]
    partners += [along_y(i) for i in range(1, SIDE)] + [along_x(i) for i in range(1, SIDE)]
    for partner in partners:
        pl.semaphore_signal(barrier, inc=1, device_id=partner, device_id_type=MESH)

    def tell(turn):
        for step in (2**turn, DEPTH - 2**turn):
            pl.semaphore_signal(near_sem.at[turn], inc=1, device_id=along_z(step), device_id_type=MESH)

    def hear(turn):
        pl.semaphore_wait(near_sem.at[turn], 2)

    def half_head(half, j):
        return pl.ds(pl.multiple_of((2 * half + j) * DK, DK), DK)

    def message(send, recv, src, dst, device):
        return pltpu.make_async_remote_copy(
            src_ref=src, dst_ref=dst, send_sem=send, recv_sem=recv, device_id=device, device_id_type=MESH
        )

    def wait_bytes(ref, sem):
        pltpu.make_async_copy(ref, ref, sem).wait()

    def sib_message(way, j):
        send, recv = send_sem.at[way, 0], sib_sem.at[way, j]
        if j == 2:
            return message(send, recv, own.at[way, pl.ds(256 * c, 256)], sib.at[way, 1], sibling)
        return message(send, recv, own.at[way, half_head(1 - c, j)], sib.at[way, 0, pl.ds(j * DK, DK)], sibling)

    def piece(half, i):
        return pl.ds(pl.multiple_of(256 * half + PIECE * i, PIECE), PIECE)

    def pref_message(way, i):
        send, recv = send_sem.at[way, 1], pref_sem.at[way, i // (PIECES // 2)]
        return message(send, recv, pref.at[way, piece(c, i)], pref.at[way, piece(c, i)], sibling)

    def base_message(way, i):
        return message(send_sem.at[way, 2], base_sem.at[way], local.at[way, i], base.at[way, i], sibling)

    def plane_message(way, phase, i, a, step):
        device = along_y(step) if phase == a else along_x(step)
        if phase == 0:
            src, dst = chip.at[way, i, a], recv1.at[way, i, a, step - 1]
        elif a == 0:
            src, dst = row.at[way, i], recv2.at[way, i, a, step - 1]
        else:
            wrapped = (y + step) // SIDE
            pick = 1 - wrapped if way == 0 else wrapped
            src, dst = cols.at[way, i, pick], recv2.at[way, i, a, step - 1]
        return message(send_sem.at[way, 3 + phase], plane_sem.at[way, phase, i], src, dst, device)

    def zmessage(step):
        return message(zsend_sem, zrecv_sem, zsend, zrecv.at[step - 1], along_z(step))

    def counts(way, step, place):
        return step <= place if way == 0 else step > place

    def start_plane(way, phase, i):
        for step in (2, 1, 3):
            for a in range(2):
                plane_message(way, phase, i, a, step).start()

    def start_first(way):
        for i in range(PIECES):
            if i % (PIECES // 2) == 0:
                sib_message(way, i // (PIECES // 2)).wait_recv()
            total = own[way, piece(c, i)] + sib[way, 0, pl.ds(PIECE * i, PIECE)]
            for a in range(2):
                chip[way, i, a] = total[PART * a : PART * a + PART]
            start_plane(way, 0, i)

    def start_second(way):
        sib_message(way, 2).wait_recv()
        for i in range(PIECES):
            wait_bytes(recv1.at[way, i], plane_sem.at[way, 0, i])
            mine = own[way, piece(1 - c, i)] + sib[way, 1, pl.ds(PIECE * i, PIECE)]
            total, before = mine[:PART], jnp.zeros((PART, DK), F32)
            column = jnp.zeros((PART, DK), F32)
            for step in range(1, SIDE):
                block = recv1[way, i, 0, step - 1]
                total = total + block
                before = before + jnp.where(counts(way, step, y), block, 0.0)
                column = column + jnp.where(counts(way, step, x), recv1[way, i, 1, step - 1], 0.0)
            row[way, i] = total
            cols[way, i, 0] = column
            cols[way, i, 1] = column + mine[PART:]
            start_plane(way, 1, i)
            local[way, i, pl.ds(0, PART)] = before
            local[way, i, pl.ds(PART, PART)] = column
            base_message(way, i).start()

    def start_third(way):
        wait_bytes(base.at[way], base_sem.at[way])
        for i in range(PIECES):
            wait_bytes(recv2.at[way, i], plane_sem.at[way, 1, i])
            first = base[way, i, pl.ds(0, PART)]
            second = base[way, i, pl.ds(PART, PART)]
            for step in range(1, SIDE):
                first = first + jnp.where(counts(way, step, x), recv2[way, i, 0, step - 1], 0.0)
                second = second + recv2[way, i, 1, step - 1]
            pref[way, piece(c, i)] = jnp.concatenate([first, second], axis=0)
            pref_message(way, i).start()

    def wait_pref(way, j):
        wait_bytes(pref.at[way, half_head(1 - c, j)], pref_sem.at[way, j])

    def leave(way):
        wait_bytes(own.at[way], send_sem.at[way, 0])
        wait_bytes(pref.at[way, pl.ds(0, 256)], send_sem.at[way, 1])
        wait_bytes(base.at[way], send_sem.at[way, 2])
        wait_bytes(recv1.at[way], send_sem.at[way, 3])
        wait_bytes(recv2.at[way], send_sem.at[way, 4])

    def state(way, mine, j):
        add = c == 1 if way == 0 else c == 0
        block = sib[way, 0 if mine else 1, pl.ds(j * DK, DK)]
        return pref[way, half_head(c if mine else 1 - c, j)] + jnp.where(add, block, 0.0)

    steps0 = lax.broadcasted_iota(jnp.int32, (DK, DK), 0)
    steps1 = lax.broadcasted_iota(jnp.int32, (DK, DK), 1)

    def causal(block, lower):
        keep = steps0 >= steps1 if lower else steps0 <= steps1
        if block.shape[1] == DK:
            return jnp.where(keep, block, 0.0).astype(BF16)
        if lower:
            cut = block.shape[1] - DK
            return jnp.concatenate(
                [block[:, :cut].astype(BF16), jnp.where(keep, block[:, cut:], 0.0).astype(BF16)], axis=1
            )
        return jnp.concatenate(
            [jnp.where(keep, block[:, :DK], 0.0).astype(BF16), block[:, DK:].astype(BF16)], axis=1
        )

    for load in loads[:2]:
        load.wait()
    for load in loads[4:]:
        load.start()
    for j in range(2):
        at = half_head(1 - c, j)
        own[0, at] = dot(k[:, at], v[:, at], TN)
    pl.semaphore_wait(barrier, len(partners))
    tell(0)
    for j in range(2):
        sib_message(0, j).start()
    for load in loads[2:4]:
        load.wait()
    for j in range(2):
        at = half_head(c, j)
        own[0, at] = dot(k[:, at], v[:, at], TN)
    sib_message(0, 2).start()
    for load in loads[4:]:
        load.wait()
    start_first(0)

    def inner(h, carry):
        at = pl.ds(pl.multiple_of(h * DK, DK), DK)
        for r in range(4):
            strip = causal(dot(q[pl.ds(r * DK, DK), at], k[pl.ds(0, (r + 1) * DK), at], NT), True)
            attn[pl.ds(r * DK, DK), at] = dot(strip, v[pl.ds(0, (r + 1) * DK), at], NN)
        return carry

    lax.fori_loop(0, HEADS_HERE, inner, 0)
    hear(0)
    tell(1)
    start_second(0)

    def prepare(h, carry):
        at = pl.ds(pl.multiple_of(h * DK, DK), DK)
        qt[at, :] = q[:, at].astype(F32).T.astype(BF16)
        for r in range(4):
            rest = ROWS - r * DK
            strip = dot(k[pl.ds(r * DK, DK), at], q[pl.ds(r * DK, rest), at], NT)
            scores_t[h, pl.ds(r * DK, DK), pl.ds(r * DK, rest)] = causal(strip, False)
        return carry

    lax.fori_loop(0, HEADS_HERE, prepare, 0)
    for h in range(HEADS_HERE):
        g[:, head(h)] = d[:, head(h)].astype(F32) * gain[h : h + 1, :].astype(F32)
    hear(1)
    tell(2)
    start_third(0)

    squares = jnp.zeros((ROWS, DK), F32)
    products = jnp.zeros((ROWS, DK), F32)
    for mine in (True, False):
        for j in range(2):
            if not mine:
                wait_pref(0, j)
            at = half_head(c if mine else 1 - c, j)
            qh = q[:, at]
            total = attn[:, at] + dot(jnp.concatenate([qh, qh], axis=1), halves(state(0, mine, j), 0), NN)
            attn[:, at] = total
            squares = squares + total * total
            products = products + total * g[:, at]

    ones = jnp.ones((8, 3 * DK), BF16)

    def row_sums(array):
        high = array.astype(BF16)
        rest = array - high.astype(F32)
        middle = rest.astype(BF16)
        low = (rest - middle.astype(F32)).astype(BF16)
        return dot(ones, jnp.concatenate([high, middle, low], axis=1), NT)

    for i, array in enumerate((squares, products)):
        sums = row_sums(array)
        for j in range(4):
            zsend[pl.ds(4 * i + j, 1), :] = sums[0:1, j * DK : (j + 1) * DK]
    hear(2)
    for step in (8, 7, 9, 6, 10, 5, 11, 4, 12, 3, 13, 2, 14, 1, 15):
        zmessage(step).start()

    leave(0)
    wait_bytes(zrecv, zrecv_sem)
    totals = zsend[...]
    for step in range(1, DEPTH):
        totals = totals + zrecv[step - 1]
    means = totals / FEATURES
    rms = jnp.sqrt(means[0:4] + 1e-05)
    inverse = 1.0 / rms
    weight = means[4:8] * inverse * inverse
    columns = jnp.concatenate([inverse, weight], axis=0).T
    for j in range(4):
        inverses[pl.ds(j * DK, DK), :] = jnp.broadcast_to(columns[:, j : j + 1], (DK, DK))
        weights[pl.ds(j * DK, DK), :] = jnp.broadcast_to(columns[:, 4 + j : 5 + j], (DK, DK))
    for mine in (False, True):
        for j in range(2):
            at = half_head(c if mine else 1 - c, j)
            delta = ((g[:, at] - attn[:, at] * weights[...]) * inverses[...]).astype(BF16)
            e[:, at] = delta
            own[1, at] = dot(qt[at, :], delta, NN)
            if not mine:
                sib_message(1, j).start()
    sib_message(1, 2).start()
    start_first(1)
    for h in range(HEADS_HERE):
        normed[:, head(h)] = (attn[:, head(h)] * inverses[...] * gain[h : h + 1, :].astype(F32)).astype(BF16)

    def outer(h, carry):
        at = pl.ds(pl.multiple_of(h * DK, DK), DK)
        for r in range(4):
            low, rest = pl.ds(r * DK, DK), ROWS - r * DK
            strip = causal(dot(v[low, at], e[pl.ds(r * DK, rest), at], NT), False)
            dk_part[low, at] = dot(strip, q[pl.ds(r * DK, rest), at], NN)
            dv_part[low, at] = dot(scores_t[h, low, pl.ds(r * DK, rest)], e[pl.ds(r * DK, rest), at], NN)
        return carry

    lax.fori_loop(0, HEADS_HERE, outer, 0)
    start_second(1)

    for mine in (True, False):
        for j in range(2):
            at = half_head(c if mine else 1 - c, j)
            back = halves(state(0, mine, j), 1)
            for r in range(4):
                low = pl.ds(r * DK, DK)
                eh = e[low, at]
                strip = causal(dot(eh, v[pl.ds(0, (r + 1) * DK), at], NT), True)
                total = dot(strip, k[pl.ds(0, (r + 1) * DK), at], NN)
                dq[low, at] = (total + dot(jnp.concatenate([eh, eh], axis=1), back, NT)).astype(BF16)
    start_third(1)
    for mine in (True, False):
        for j in range(2):
            at = half_head(c if mine else 1 - c, j)
            if mine:
                last_products(at, state(1, mine, j), k, v, dk_part, dv_part, dk, dv)
            else:
                wait_pref(1, j)
                later[pl.ds(j * DK, DK)] = state(1, mine, j)

    leave(1)
    wait_bytes(zrecv, zsend_sem)


def last_products(at, back, k, v, dk_part, dv_part, dk, dv):
    vh, kh = v[:, at], k[:, at]
    total = dk_part[:, at] + dot(jnp.concatenate([vh, vh], axis=1), halves(back, 1), NT)
    dk[:, at] = total.astype(BF16)
    total = dv_part[:, at] + dot(jnp.concatenate([kh, kh], axis=1), halves(back, 0), NN)
    dv[:, at] = total.astype(BF16)


def finish(
    normed, dq, dk_mine, dv_mine, dk_part, dv_part, later, k, v,
    normed_hbm, dq_hbm, dk_hbm, dv_hbm,
    dk, dv, store_sem,
):
    c = lax.axis_index("seq") % 2
    stores = []

    def store(src, dst):
        copy = pltpu.make_async_copy(src, dst, store_sem.at[len(stores)])
        copy.start()
        stores.append(copy)

    here = pl.ds(pl.multiple_of(256 * c, 256), 256)
    store(dk_mine.at[:, here], dk_hbm.at[:, here])
    store(dv_mine.at[:, here], dv_hbm.at[:, here])
    for part in range(2):
        rows = pl.ds(256 * part, 256)
        store(normed.at[rows], normed_hbm.at[rows])
        store(dq.at[rows], dq_hbm.at[rows])
    for j in range(2):
        at = pl.ds(pl.multiple_of((2 * (1 - c) + j) * DK, DK), DK)
        last_products(at, later[pl.ds(j * DK, DK)], k, v, dk_part, dv_part, dk, dv)
        store(dk.at[:, at], dk_hbm.at[:, at])
        store(dv.at[:, at], dv_hbm.at[:, at])
    for copy in stores:
        copy.wait()


def shards(queries, keys, values, gain, d_out):
    width = HEADS_HERE * DK
    block = pltpu.VMEM((ROWS, width), BF16)
    wide = pltpu.VMEM((ROWS, width), F32)
    states = pltpu.VMEM((256, DK), F32)
    in_hbm = pl.BlockSpec(memory_space=pltpu.HBM)
    in_vmem = pl.BlockSpec(memory_space=pltpu.VMEM)
    arguments = (queries, keys, values, gain.reshape(HEADS_HERE, DK), d_out)
    partial = pl.pallas_call(
        body,
        out_shape=[block, block, block, block, wide, wide, states, block, block],
        in_specs=[in_hbm] * 5,
        out_specs=[in_vmem] * 9,
        scratch_shapes=[
            block, block, pltpu.VMEM((HEADS_HERE, DK), BF16),
            pltpu.VMEM((width, ROWS), BF16),
            pltpu.VMEM((HEADS_HERE, ROWS, ROWS), BF16),
            wide, wide, block, pltpu.VMEM((ROWS, DK), F32), pltpu.VMEM((ROWS, DK), F32),
            pltpu.VMEM((2, width, DK), F32),
            pltpu.VMEM((2, 2, 256, DK), F32),
            pltpu.VMEM((2, PIECES, 2, PART, DK), F32),
            pltpu.VMEM((2, PIECES, 2, 3, PART, DK), F32),
            pltpu.VMEM((2, PIECES, PART, DK), F32),
            pltpu.VMEM((2, PIECES, 2, PART, DK), F32),
            pltpu.VMEM((2, PIECES, PIECE, DK), F32),
            pltpu.VMEM((2, PIECES, PIECE, DK), F32),
            pltpu.VMEM((2, PIECES, 2, 3, PART, DK), F32),
            pltpu.VMEM((2, width, DK), F32),
            pltpu.VMEM((8, DK), F32),
            pltpu.VMEM((DEPTH - 1, 8, DK), F32),
            pltpu.SemaphoreType.DMA((7,)),
            pltpu.SemaphoreType.DMA((2, 5)),
            pltpu.SemaphoreType.DMA((2, 3)),
            pltpu.SemaphoreType.DMA((2, 2)),
            pltpu.SemaphoreType.DMA((2,)),
            pltpu.SemaphoreType.DMA((2, 2, PIECES)),
            pltpu.SemaphoreType.DMA,
            pltpu.SemaphoreType.DMA,
            pltpu.SemaphoreType.REGULAR((3,)),
        ],
        compiler_params=pltpu.CompilerParams(
            collective_id=0, has_side_effects=True, vmem_limit_bytes=32 * 1024 * 1024
        ),
        name="attention",
    )(*[pltpu.with_memory_space_constraint(array, pltpu.HBM) for array in arguments])
    return pl.pallas_call(
        finish,
        out_shape=[jax.ShapeDtypeStruct((ROWS, width), BF16)] * 4,
        in_specs=[in_vmem] * 9,
        out_specs=[in_hbm] * 4,
        scratch_shapes=[block, block, pltpu.SemaphoreType.DMA((10,))],
        compiler_params=pltpu.CompilerParams(vmem_limit_bytes=16 * 1024 * 1024),
        name="finish",
    )(*[pltpu.with_memory_space_constraint(array, pltpu.VMEM) for array in partial])


def solution(mesh):
    in_specs = (P("seq", "head"), P("seq", "head"), P("seq", "head"), P("head"), P("seq", "head"))
    out_specs = (P("seq", "head"), P("seq", "head"), P("seq", "head"), P("seq", "head"))
    return jax.shard_map(shards, mesh=mesh, in_specs=in_specs, out_specs=out_specs, check_vma=False)
```

```python
import functools

import jax
import jax.numpy as jnp
from jax import lax
from jax.experimental import pallas as pl
from jax.experimental.pallas import tpu as pltpu
from jax.sharding import PartitionSpec as P

DK = 128
ROWS = 512
HEADS_HERE = 4
PIECES = 4
PIECE = 256 // PIECES
PART = PIECE // 2
FEATURES = 8192
SIDE = 4
DEPTH = 16
MESH = pl.DeviceIdType.MESH
F32 = jnp.float32
BF16 = jnp.bfloat16

NN = (((1,), (0,)), ((), ()))
NT = (((1,), (1,)), ((), ()))
TN = (((0,), (0,)), ((), ()))


def dot(left, right, dims):
    return lax.dot_general(left, right, dims, preferred_element_type=F32)


def head(h):
    return pl.ds(h * DK, DK)


def halves(state, axis):
    high = state.astype(BF16)
    low = (state - high.astype(F32)).astype(BF16)
    return jnp.concatenate([high, low], axis=axis)


def body(
    q_hbm, k_hbm, v_hbm, gain_hbm, d_hbm,
    normed, dq, dk, dv, dk_part, dv_part, later, k, v,
    q, d, gain,
    qt, scores_t, attn, g, e, inverses, weights,
    own, sib, chip, recv1, row, cols, local, recv2, pref,
    zsend, zrecv,
    load_sem, send_sem, sib_sem, pref_sem, plane_sem, zsend_sem, zrecv_sem, near_sem, plane_near_sem,
):
    s = lax.axis_index("seq")
    z = lax.axis_index("head")
    x, y, c = s // 8, (s // 2) % SIDE, s % 2
    sibling = (s + 1 - 2 * c, z)

    def along_y(step):
        return (x * 8 + ((y + step) % SIDE) * 2 + c, z)

    def along_x(step):
        return (((x + step) % SIDE) * 8 + y * 2 + c, z)

    def along_z(step):
        return (s, (z + step) % DEPTH)

    here, there = pl.ds(pl.multiple_of(256 * c, 256), 256), pl.ds(pl.multiple_of(256 - 256 * c, 256), 256)
    loads = [
        pltpu.make_async_copy(src, dst, load_sem.at[i])
        for i, (src, dst) in enumerate(
            (
                (k_hbm.at[:, there], k.at[:, there]),
                (v_hbm.at[:, there], v.at[:, there]),
                (k_hbm.at[:, here], k.at[:, here]),
                (v_hbm.at[:, here], v.at[:, here]),
                (q_hbm, q),
                (d_hbm, d),
                (gain_hbm, gain),
            )
        )
    ]
    barrier = pltpu.get_barrier_semaphore()
    partners = [sibling, along_z(1), along_z(DEPTH - 1)]
    partners += [along_y(1), along_y(SIDE - 1), along_x(1), along_x(SIDE - 1)]
    for partner in partners:
        pl.semaphore_signal(barrier, inc=1, device_id=partner, device_id_type=MESH)
    for load in loads[:4]:
        load.start()

    def tell(turn):
        for step in (2**turn, DEPTH - 2**turn):
            pl.semaphore_signal(near_sem.at[turn], inc=1, device_id=along_z(step), device_id_type=MESH)

    def hear(turn):
        pl.semaphore_wait(near_sem.at[turn], 2)

    def tell_plane():
        for device in (along_y(SIDE - 1), along_x(SIDE - 1)):
            pl.semaphore_signal(plane_near_sem, inc=1, device_id=device, device_id_type=MESH)

    def half_head(half, j):
        return pl.ds(pl.multiple_of((2 * half + j) * DK, DK), DK)

    def message(send, recv, src, dst, device):
        return pltpu.make_async_remote_copy(
            src_ref=src, dst_ref=dst, send_sem=send, recv_sem=recv, device_id=device, device_id_type=MESH
        )

    def wait_bytes(ref, sem):
        pltpu.make_async_copy(ref, ref, sem).wait()

    def sib_message(way, j):
        send, recv = send_sem.at[way, 0], sib_sem.at[way, j]
        if j == 2:
            return message(send, recv, own.at[way, pl.ds(256 * c, 256)], sib.at[way, 1], sibling)
        return message(send, recv, own.at[way, half_head(1 - c, j)], sib.at[way, 0, pl.ds(j * DK, DK)], sibling)

    def piece(half, i):
        return pl.ds(pl.multiple_of(256 * half + PIECE * i, PIECE), PIECE)

    def pref_message(way, j):
        at = half_head(c, j)
        return message(send_sem.at[way, 1], pref_sem.at[way, j], pref.at[way, at], pref.at[way, at], sibling)

    def plane_message(way, phase, i, a, step):
        device = along_y(step) if phase == a else along_x(step)
        if phase == 0:
            src, dst = chip.at[way, i, a], recv1.at[way, i, a, step - 1]
        elif a == 0:
            src, dst = row.at[way, i], recv2.at[way, i, a, step - 1]
        else:
            wrapped = (y + step) // SIDE
            pick = 1 - wrapped if way == 0 else wrapped
            src, dst = cols.at[way, i, pick], recv2.at[way, i, a, step - 1]
        return message(send_sem.at[way, 2 + phase], plane_sem.at[way, phase, i], src, dst, device)

    def zmessage(step):
        return message(zsend_sem, zrecv_sem, zsend, zrecv.at[step - 1], along_z(step))

    def counts(way, step, place):
        return step <= place if way == 0 else step > place

    def start_plane(way, phase, i):
        for step in (2, 1, 3):
            for a in range(2):
                plane_message(way, phase, i, a, step).start()

    def start_first(way):
        for i in range(PIECES):
            if i % (PIECES // 2) == 0:
                sib_message(way, i // (PIECES // 2)).wait_recv()
            total = own[way, piece(c, i)] + sib[way, 0, pl.ds(PIECE * i, PIECE)]
            for a in range(2):
                chip[way, i, a] = total[PART * a : PART * a + PART]
            start_plane(way, 0, i)

    def start_second(way):
        for i in range(PIECES):
            wait_bytes(recv1.at[way, i], plane_sem.at[way, 0, i])
            total, before = chip[way, i, 0], jnp.zeros((PART, DK), F32)
            column = jnp.zeros((PART, DK), F32)
            for step in range(1, SIDE):
                block = recv1[way, i, 0, step - 1]
                total = total + block
                before = before + jnp.where(counts(way, step, y), block, 0.0)
                column = column + jnp.where(counts(way, step, x), recv1[way, i, 1, step - 1], 0.0)
            row[way, i] = total
            cols[way, i, 0] = column
            cols[way, i, 1] = column + chip[way, i, 1]
            start_plane(way, 1, i)
            local[way, i, pl.ds(0, PART)] = before
            local[way, i, pl.ds(PART, PART)] = column

    def start_third(way):
        sib_message(way, 2).wait_recv()
        for i in range(PIECES):
            wait_bytes(recv2.at[way, i], plane_sem.at[way, 1, i])
            first = local[way, i, pl.ds(0, PART)]
            second = local[way, i, pl.ds(PART, PART)]
            for step in range(1, SIDE):
                first = first + jnp.where(counts(way, step, x), recv2[way, i, 0, step - 1], 0.0)
                second = second + recv2[way, i, 1, step - 1]
            pref[way, piece(c, i)] = jnp.concatenate([first, second], axis=0)
            if (i + 1) % (PIECES // 2) == 0:
                pref_message(way, i // (PIECES // 2)).start()

    def wait_pref(way, j):
        wait_bytes(pref.at[way, half_head(1 - c, j)], pref_sem.at[way, j])

    def leave(way):
        wait_bytes(own.at[way], send_sem.at[way, 0])
        wait_bytes(pref.at[way, pl.ds(0, 256)], send_sem.at[way, 1])
        wait_bytes(recv1.at[way], send_sem.at[way, 2])
        wait_bytes(recv2.at[way], send_sem.at[way, 3])

    def state(way, mine, j):
        add = c == 1 if way == 0 else c == 0
        block = sib[way, 0 if mine else 1, pl.ds(j * DK, DK)]
        return pref[way, half_head(c if mine else 1 - c, j)] + jnp.where(add, block, 0.0)

    steps0 = lax.broadcasted_iota(jnp.int32, (DK, DK), 0)
    steps1 = lax.broadcasted_iota(jnp.int32, (DK, DK), 1)

    def causal(block, lower):
        keep = steps0 >= steps1 if lower else steps0 <= steps1
        if block.shape[1] == DK:
            return jnp.where(keep, block, 0.0).astype(BF16)
        if lower:
            cut = block.shape[1] - DK
            return jnp.concatenate(
                [block[:, :cut].astype(BF16), jnp.where(keep, block[:, cut:], 0.0).astype(BF16)], axis=1
            )
        return jnp.concatenate(
            [jnp.where(keep, block[:, :DK], 0.0).astype(BF16), block[:, DK:].astype(BF16)], axis=1
        )

    for load in loads[:2]:
        load.wait()
    for load in loads[4:]:
        load.start()
    for j in range(2):
        at = half_head(1 - c, j)
        own[0, at] = dot(k[:, at], v[:, at], TN)
    pl.semaphore_wait(barrier, len(partners))
    tell_plane()
    tell(0)
    for j in range(2):
        sib_message(0, j).start()
    for load in loads[2:4]:
        load.wait()
    for j in range(2):
        at = half_head(c, j)
        own[0, at] = dot(k[:, at], v[:, at], TN)
    sib_message(0, 2).start()
    pl.semaphore_wait(plane_near_sem, 2)
    start_first(0)
    for load in loads[4:]:
        load.wait()

    def inner(h, carry):
        at = pl.ds(pl.multiple_of(h * DK, DK), DK)
        for r in range(4):
            strip = causal(dot(q[pl.ds(r * DK, DK), at], k[pl.ds(0, (r + 1) * DK), at], NT), True)
            attn[pl.ds(r * DK, DK), at] = dot(strip, v[pl.ds(0, (r + 1) * DK), at], NN)
        return carry

    lax.fori_loop(0, HEADS_HERE, inner, 0)
    hear(0)
    tell(1)
    start_second(0)

    def prepare(h, carry):
        at = pl.ds(pl.multiple_of(h * DK, DK), DK)
        qt[at, :] = q[:, at].astype(F32).T.astype(BF16)
        for r in range(4):
            rest = ROWS - r * DK
            strip = dot(k[pl.ds(r * DK, DK), at], q[pl.ds(r * DK, rest), at], NT)
            scores_t[h, pl.ds(r * DK, DK), pl.ds(r * DK, rest)] = causal(strip, False)
        return carry

    lax.fori_loop(0, HEADS_HERE, prepare, 0)
    for h in range(HEADS_HERE):
        g[:, head(h)] = d[:, head(h)].astype(F32) * gain[h : h + 1, :].astype(F32)
    hear(1)
    tell(2)
    start_third(0)

    squares = jnp.zeros((ROWS, DK), F32)
    products = jnp.zeros((ROWS, DK), F32)
    for mine in (True, False):
        for j in range(2):
            if not mine:
                wait_pref(0, j)
            at = half_head(c if mine else 1 - c, j)
            qh = q[:, at]
            total = attn[:, at] + dot(jnp.concatenate([qh, qh], axis=1), halves(state(0, mine, j), 0), NN)
            attn[:, at] = total
            squares = squares + total * total
            products = products + total * g[:, at]

    ones = jnp.ones((8, 3 * DK), BF16)

    def row_sums(array):
        high = array.astype(BF16)
        rest = array - high.astype(F32)
        middle = rest.astype(BF16)
        low = (rest - middle.astype(F32)).astype(BF16)
        return dot(ones, jnp.concatenate([high, middle, low], axis=1), NT)

    for i, array in enumerate((squares, products)):
        sums = row_sums(array)
        for j in range(4):
            zsend[pl.ds(4 * i + j, 1), :] = sums[0:1, j * DK : (j + 1) * DK]
    hear(2)
    for step in (8, 7, 9, 6, 10, 5, 11, 4, 12, 3, 13, 2, 14, 1, 15):
        zmessage(step).start()

    leave(0)
    wait_bytes(zrecv, zrecv_sem)
    totals = zsend[...]
    for step in range(1, DEPTH):
        totals = totals + zrecv[step - 1]
    means = totals / FEATURES
    rms = jnp.sqrt(means[0:4] + 1e-05)
    inverse = 1.0 / rms
    weight = means[4:8] * inverse * inverse
    columns = jnp.concatenate([inverse, weight], axis=0).T
    for j in range(4):
        inverses[pl.ds(j * DK, DK), :] = jnp.broadcast_to(columns[:, j : j + 1], (DK, DK))
        weights[pl.ds(j * DK, DK), :] = jnp.broadcast_to(columns[:, 4 + j : 5 + j], (DK, DK))
    for mine in (False, True):
        for j in range(2):
            at = half_head(c if mine else 1 - c, j)
            delta = ((g[:, at] - attn[:, at] * weights[...]) * inverses[...]).astype(BF16)
            e[:, at] = delta
            own[1, at] = dot(qt[at, :], delta, NN)
            if not mine:
                sib_message(1, j).start()
    sib_message(1, 2).start()
    start_first(1)
    for h in range(HEADS_HERE):
        normed[:, head(h)] = (attn[:, head(h)] * inverses[...] * gain[h : h + 1, :].astype(F32)).astype(BF16)

    def outer(h, carry):
        at = pl.ds(pl.multiple_of(h * DK, DK), DK)
        for r in range(4):
            low, rest = pl.ds(r * DK, DK), ROWS - r * DK
            strip = causal(dot(v[low, at], e[pl.ds(r * DK, rest), at], NT), False)
            dk_part[low, at] = dot(strip, q[pl.ds(r * DK, rest), at], NN)
            dv_part[low, at] = dot(scores_t[h, low, pl.ds(r * DK, rest)], e[pl.ds(r * DK, rest), at], NN)
        return carry

    lax.fori_loop(0, HEADS_HERE, outer, 0)
    start_second(1)

    for mine in (True, False):
        for j in range(2):
            at = half_head(c if mine else 1 - c, j)
            back = halves(state(0, mine, j), 1)
            for r in range(4):
                low = pl.ds(r * DK, DK)
                eh = e[low, at]
                strip = causal(dot(eh, v[pl.ds(0, (r + 1) * DK), at], NT), True)
                total = dot(strip, k[pl.ds(0, (r + 1) * DK), at], NN)
                dq[low, at] = (total + dot(jnp.concatenate([eh, eh], axis=1), back, NT)).astype(BF16)
    start_third(1)
    for mine in (True, False):
        for j in range(2):
            at = half_head(c if mine else 1 - c, j)
            if mine:
                last_products(at, state(1, mine, j), k, v, dk_part, dv_part, dk, dv)
            else:
                wait_pref(1, j)
                later[pl.ds(j * DK, DK)] = state(1, mine, j)

    leave(1)
    wait_bytes(zrecv, zsend_sem)


def last_products(at, back, k, v, dk_part, dv_part, dk, dv):
    vh, kh = v[:, at], k[:, at]
    total = dk_part[:, at] + dot(jnp.concatenate([vh, vh], axis=1), halves(back, 1), NT)
    dk[:, at] = total.astype(BF16)
    total = dv_part[:, at] + dot(jnp.concatenate([kh, kh], axis=1), halves(back, 0), NN)
    dv[:, at] = total.astype(BF16)


def finish(
    normed, dq, dk_mine, dv_mine, dk_part, dv_part, later, k, v,
    normed_hbm, dq_hbm, dk_hbm, dv_hbm,
    dk, dv, store_sem,
):
    c = lax.axis_index("seq") % 2
    stores = []

    def store(src, dst):
        copy = pltpu.make_async_copy(src, dst, store_sem.at[len(stores)])
        copy.start()
        stores.append(copy)

    here = pl.ds(pl.multiple_of(256 * c, 256), 256)
    store(dk_mine.at[:, here], dk_hbm.at[:, here])
    store(dv_mine.at[:, here], dv_hbm.at[:, here])
    for part in range(2):
        rows = pl.ds(256 * part, 256)
        store(normed.at[rows], normed_hbm.at[rows])
        store(dq.at[rows], dq_hbm.at[rows])
    for j in range(2):
        at = pl.ds(pl.multiple_of((2 * (1 - c) + j) * DK, DK), DK)
        last_products(at, later[pl.ds(j * DK, DK)], k, v, dk_part, dv_part, dk, dv)
        store(dk.at[:, at], dk_hbm.at[:, at])
        store(dv.at[:, at], dv_hbm.at[:, at])
    for copy in stores:
        copy.wait()


def shards(queries, keys, values, gain, d_out):
    width = HEADS_HERE * DK
    block = pltpu.VMEM((ROWS, width), BF16)
    wide = pltpu.VMEM((ROWS, width), F32)
    states = pltpu.VMEM((256, DK), F32)
    in_hbm = pl.BlockSpec(memory_space=pltpu.HBM)
    in_vmem = pl.BlockSpec(memory_space=pltpu.VMEM)
    arguments = (queries, keys, values, gain.reshape(HEADS_HERE, DK), d_out)
    partial = pl.pallas_call(
        body,
        out_shape=[block, block, block, block, wide, wide, states, block, block],
        in_specs=[in_hbm] * 5,
        out_specs=[in_vmem] * 9,
        scratch_shapes=[
            block, block, pltpu.VMEM((HEADS_HERE, DK), BF16),
            pltpu.VMEM((width, ROWS), BF16),
            pltpu.VMEM((HEADS_HERE, ROWS, ROWS), BF16),
            wide, wide, block, pltpu.VMEM((ROWS, DK), F32), pltpu.VMEM((ROWS, DK), F32),
            pltpu.VMEM((2, width, DK), F32),
            pltpu.VMEM((2, 2, 256, DK), F32),
            pltpu.VMEM((2, PIECES, 2, PART, DK), F32),
            pltpu.VMEM((2, PIECES, 2, 3, PART, DK), F32),
            pltpu.VMEM((2, PIECES, PART, DK), F32),
            pltpu.VMEM((2, PIECES, 2, PART, DK), F32),
            pltpu.VMEM((2, PIECES, PIECE, DK), F32),
            pltpu.VMEM((2, PIECES, 2, 3, PART, DK), F32),
            pltpu.VMEM((2, width, DK), F32),
            pltpu.VMEM((8, DK), F32),
            pltpu.VMEM((DEPTH - 1, 8, DK), F32),
            pltpu.SemaphoreType.DMA((7,)),
            pltpu.SemaphoreType.DMA((2, 4)),
            pltpu.SemaphoreType.DMA((2, 3)),
            pltpu.SemaphoreType.DMA((2, 2)),
            pltpu.SemaphoreType.DMA((2, 2, PIECES)),
            pltpu.SemaphoreType.DMA,
            pltpu.SemaphoreType.DMA,
            pltpu.SemaphoreType.REGULAR((3,)),
            pltpu.SemaphoreType.REGULAR,
        ],
        compiler_params=pltpu.CompilerParams(
            collective_id=0, has_side_effects=True, vmem_limit_bytes=32 * 1024 * 1024
        ),
        name="attention",
    )(*[pltpu.with_memory_space_constraint(array, pltpu.HBM) for array in arguments])
    return pl.pallas_call(
        finish,
        out_shape=[jax.ShapeDtypeStruct((ROWS, width), BF16)] * 4,
        in_specs=[in_vmem] * 9,
        out_specs=[in_hbm] * 4,
        scratch_shapes=[block, block, pltpu.SemaphoreType.DMA((10,))],
        compiler_params=pltpu.CompilerParams(vmem_limit_bytes=16 * 1024 * 1024),
        name="finish",
    )(*[pltpu.with_memory_space_constraint(array, pltpu.VMEM) for array in partial])


def solution(mesh):
    in_specs = (P("seq", "head"), P("seq", "head"), P("seq", "head"), P("head"), P("seq", "head"))
    out_specs = (P("seq", "head"), P("seq", "head"), P("seq", "head"), P("seq", "head"))
    return jax.shard_map(shards, mesh=mesh, in_specs=in_specs, out_specs=out_specs, check_vma=False)
```

```python
import functools

import jax
import jax.numpy as jnp
from jax import lax
from jax.experimental import pallas as pl
from jax.experimental.pallas import tpu as pltpu
from jax.sharding import PartitionSpec as P

DK = 128
ROWS = 512
HEADS_HERE = 4
PIECES = 4
PIECE = 256 // PIECES
PART = PIECE // 2
FEATURES = 8192
SIDE = 4
DEPTH = 16
MESH = pl.DeviceIdType.MESH
F32 = jnp.float32
BF16 = jnp.bfloat16

NN = (((1,), (0,)), ((), ()))
NT = (((1,), (1,)), ((), ()))
TN = (((0,), (0,)), ((), ()))


def dot(left, right, dims):
    return lax.dot_general(left, right, dims, preferred_element_type=F32)


def head(h):
    return pl.ds(h * DK, DK)


def halves(state, axis):
    high = state.astype(BF16)
    low = (state - high.astype(F32)).astype(BF16)
    return jnp.concatenate([high, low], axis=axis)


def body(
    q_hbm, k_hbm, v_hbm, gain, d_hbm,
    normed, dq, dk, dv, dk_part, dv_part, later, k, v,
    q, d,
    qt, scores_t, attn, g, e, inverses, weights,
    own, sib, chip, recv1, row, cols, local, recv2, pref,
    zsend, zrecv,
    load_sem, send_sem, sib_sem, pref_sem, plane_sem, zsend_sem, zrecv_sem, near_sem, plane_near_sem,
):
    s = lax.axis_index("seq")
    z = lax.axis_index("head")
    x, y, c = s // 8, (s // 2) % SIDE, s % 2
    sibling = (s + 1 - 2 * c, z)

    def along_y(step):
        return (x * 8 + ((y + step) % SIDE) * 2 + c, z)

    def along_x(step):
        return (((x + step) % SIDE) * 8 + y * 2 + c, z)

    def along_z(step):
        return (s, (z + step) % DEPTH)

    here, there = pl.ds(pl.multiple_of(256 * c, 256), 256), pl.ds(pl.multiple_of(256 - 256 * c, 256), 256)
    loads = [
        pltpu.make_async_copy(src, dst, load_sem.at[i])
        for i, (src, dst) in enumerate(
            (
                (k_hbm.at[:, there], k.at[:, there]),
                (v_hbm.at[:, there], v.at[:, there]),
                (k_hbm.at[:, here], k.at[:, here]),
                (v_hbm.at[:, here], v.at[:, here]),
                (q_hbm, q),
                (d_hbm, d),
            )
        )
    ]
    barrier = pltpu.get_barrier_semaphore()
    partners = [sibling, along_z(1), along_z(DEPTH - 1)]
    partners += [along_y(1), along_y(SIDE - 1), along_x(1), along_x(SIDE - 1)]
    for partner in partners:
        pl.semaphore_signal(barrier, inc=1, device_id=partner, device_id_type=MESH)
    for load in loads[:4]:
        load.start()

    def tell(turn):
        for step in (2**turn, DEPTH - 2**turn):
            pl.semaphore_signal(near_sem.at[turn], inc=1, device_id=along_z(step), device_id_type=MESH)

    def hear(turn):
        pl.semaphore_wait(near_sem.at[turn], 2)

    def tell_plane():
        for device in (along_y(SIDE - 1), along_x(SIDE - 1)):
            pl.semaphore_signal(plane_near_sem, inc=1, device_id=device, device_id_type=MESH)

    def half_head(half, j):
        return pl.ds(pl.multiple_of((2 * half + j) * DK, DK), DK)

    def message(send, recv, src, dst, device):
        return pltpu.make_async_remote_copy(
            src_ref=src, dst_ref=dst, send_sem=send, recv_sem=recv, device_id=device, device_id_type=MESH
        )

    def wait_bytes(ref, sem):
        pltpu.make_async_copy(ref, ref, sem).wait()

    def sib_message(way, j):
        send, recv = send_sem.at[way, 0], sib_sem.at[way, j]
        if j == 2:
            return message(send, recv, own.at[way, pl.ds(256 * c, 256)], sib.at[way, 1], sibling)
        return message(send, recv, own.at[way, half_head(1 - c, j)], sib.at[way, 0, pl.ds(j * DK, DK)], sibling)

    def piece(half, i):
        return pl.ds(pl.multiple_of(256 * half + PIECE * i, PIECE), PIECE)

    def pref_message(way, j):
        at = half_head(c, j)
        return message(send_sem.at[way, 1], pref_sem.at[way, j], pref.at[way, at], pref.at[way, at], sibling)

    def plane_message(way, phase, i, a, step):
        device = along_y(step) if phase == a else along_x(step)
        if phase == 0:
            src, dst = chip.at[way, i, a], recv1.at[way, i, a, step - 1]
        elif a == 0:
            src, dst = row.at[way, i], recv2.at[way, i, a, step - 1]
        else:
            wrapped = (y + step) // SIDE
            pick = 1 - wrapped if way == 0 else wrapped
            src, dst = cols.at[way, i, pick], recv2.at[way, i, a, step - 1]
        return message(send_sem.at[way, 2 + phase], plane_sem.at[way, phase, i], src, dst, device)

    def zmessage(step):
        return message(zsend_sem, zrecv_sem, zsend, zrecv.at[step - 1], along_z(step))

    def counts(way, step, place):
        return step <= place if way == 0 else step > place

    def start_plane(way, phase, i):
        for step in (2, 1, 3):
            for a in range(2):
                plane_message(way, phase, i, a, step).start()

    def start_first(way):
        for i in range(PIECES):
            if i % (PIECES // 2) == 0:
                sib_message(way, i // (PIECES // 2)).wait_recv()
            total = own[way, piece(c, i)] + sib[way, 0, pl.ds(PIECE * i, PIECE)]
            for a in range(2):
                chip[way, i, a] = total[PART * a : PART * a + PART]
            start_plane(way, 0, i)

    def start_second(way):
        for i in range(PIECES):
            wait_bytes(recv1.at[way, i], plane_sem.at[way, 0, i])
            total, before = chip[way, i, 0], jnp.zeros((PART, DK), F32)
            column = jnp.zeros((PART, DK), F32)
            for step in range(1, SIDE):
                total = total + recv1[way, i, 0, step - 1]
                column = column + jnp.where(counts(way, step, x), recv1[way, i, 1, step - 1], 0.0)
            row[way, i] = total
            cols[way, i, 0] = column
            cols[way, i, 1] = column + chip[way, i, 1]
            start_plane(way, 1, i)
            for step in range(1, SIDE):
                before = before + jnp.where(counts(way, step, y), recv1[way, i, 0, step - 1], 0.0)
            local[way, i, pl.ds(0, PART)] = before
            local[way, i, pl.ds(PART, PART)] = column

    def start_third(way):
        sib_message(way, 2).wait_recv()
        for i in range(PIECES):
            wait_bytes(recv2.at[way, i], plane_sem.at[way, 1, i])
            first = local[way, i, pl.ds(0, PART)]
            second = local[way, i, pl.ds(PART, PART)]
            for step in range(1, SIDE):
                first = first + jnp.where(counts(way, step, x), recv2[way, i, 0, step - 1], 0.0)
                second = second + recv2[way, i, 1, step - 1]
            pref[way, piece(c, i)] = jnp.concatenate([first, second], axis=0)
            if (i + 1) % (PIECES // 2) == 0:
                pref_message(way, i // (PIECES // 2)).start()

    def wait_pref(way, j):
        wait_bytes(pref.at[way, half_head(1 - c, j)], pref_sem.at[way, j])

    def leave(way):
        wait_bytes(own.at[way], send_sem.at[way, 0])
        wait_bytes(pref.at[way, pl.ds(0, 256)], send_sem.at[way, 1])
        wait_bytes(recv1.at[way], send_sem.at[way, 2])
        wait_bytes(recv2.at[way], send_sem.at[way, 3])

    def state(way, mine, j):
        add = c == 1 if way == 0 else c == 0
        block = sib[way, 0 if mine else 1, pl.ds(j * DK, DK)]
        return pref[way, half_head(c if mine else 1 - c, j)] + jnp.where(add, block, 0.0)

    steps0 = lax.broadcasted_iota(jnp.int32, (DK, DK), 0)
    steps1 = lax.broadcasted_iota(jnp.int32, (DK, DK), 1)

    def causal(block, lower):
        keep = steps0 >= steps1 if lower else steps0 <= steps1
        if block.shape[1] == DK:
            return jnp.where(keep, block, 0.0).astype(BF16)
        if lower:
            cut = block.shape[1] - DK
            return jnp.concatenate(
                [block[:, :cut].astype(BF16), jnp.where(keep, block[:, cut:], 0.0).astype(BF16)], axis=1
            )
        return jnp.concatenate(
            [jnp.where(keep, block[:, :DK], 0.0).astype(BF16), block[:, DK:].astype(BF16)], axis=1
        )

    for load in loads[:2]:
        load.wait()
    for load in loads[4:]:
        load.start()
    for j in range(2):
        at = half_head(1 - c, j)
        own[0, at] = dot(k[:, at], v[:, at], TN)
    pl.semaphore_wait(barrier, len(partners))
    tell_plane()
    tell(0)
    for j in range(2):
        sib_message(0, j).start()
    for load in loads[2:4]:
        load.wait()
    for j in range(2):
        at = half_head(c, j)
        own[0, at] = dot(k[:, at], v[:, at], TN)
    sib_message(0, 2).start()
    pl.semaphore_wait(plane_near_sem, 2)
    start_first(0)
    for load in loads[4:]:
        load.wait()

    def inner(h, carry):
        at = pl.ds(pl.multiple_of(h * DK, DK), DK)
        for r in range(4):
            strip = causal(dot(q[pl.ds(r * DK, DK), at], k[pl.ds(0, (r + 1) * DK), at], NT), True)
            attn[pl.ds(r * DK, DK), at] = dot(strip, v[pl.ds(0, (r + 1) * DK), at], NN)
        return carry

    lax.fori_loop(0, HEADS_HERE, inner, 0)
    hear(0)
    tell(1)
    start_second(0)

    def prepare(h, carry):
        at = pl.ds(pl.multiple_of(h * DK, DK), DK)
        qt[at, :] = q[:, at].astype(F32).T.astype(BF16)
        for r in range(4):
            rest = ROWS - r * DK
            strip = dot(k[pl.ds(r * DK, DK), at], q[pl.ds(r * DK, rest), at], NT)
            scores_t[h, pl.ds(r * DK, DK), pl.ds(r * DK, rest)] = causal(strip, False)
        return carry

    lax.fori_loop(0, HEADS_HERE, prepare, 0)
    for h in range(HEADS_HERE):
        g[:, head(h)] = d[:, head(h)].astype(F32) * gain[h : h + 1, :]
    hear(1)
    tell(2)
    start_third(0)

    squares = jnp.zeros((ROWS, DK), F32)
    products = jnp.zeros((ROWS, DK), F32)
    for mine in (True, False):
        for j in range(2):
            if not mine:
                wait_pref(0, j)
            at = half_head(c if mine else 1 - c, j)
            qh = q[:, at]
            total = attn[:, at] + dot(jnp.concatenate([qh, qh], axis=1), halves(state(0, mine, j), 0), NN)
            attn[:, at] = total
            squares = squares + total * total
            products = products + total * g[:, at]

    ones = jnp.ones((8, 3 * DK), BF16)

    def row_sums(array):
        high = array.astype(BF16)
        rest = array - high.astype(F32)
        middle = rest.astype(BF16)
        low = (rest - middle.astype(F32)).astype(BF16)
        return dot(ones, jnp.concatenate([high, middle, low], axis=1), NT)

    for i, array in enumerate((squares, products)):
        sums = row_sums(array)
        for j in range(4):
            zsend[pl.ds(4 * i + j, 1), :] = sums[0:1, j * DK : (j + 1) * DK]
    hear(2)
    for step in (8, 7, 9, 6, 10, 5, 11, 4, 12, 3, 13, 2, 14, 1, 15):
        zmessage(step).start()

    leave(0)
    wait_bytes(zrecv, zrecv_sem)
    totals = zsend[...]
    for step in range(1, DEPTH):
        totals = totals + zrecv[step - 1]
    means = totals / FEATURES
    rms = jnp.sqrt(means[0:4] + 1e-05)
    inverse = 1.0 / rms
    weight = means[4:8] * inverse * inverse
    columns = jnp.concatenate([inverse, weight], axis=0).T
    for j in range(4):
        inverses[pl.ds(j * DK, DK), :] = jnp.broadcast_to(columns[:, j : j + 1], (DK, DK))
        weights[pl.ds(j * DK, DK), :] = jnp.broadcast_to(columns[:, 4 + j : 5 + j], (DK, DK))
    for mine in (False, True):
        for j in range(2):
            at = half_head(c if mine else 1 - c, j)
            delta = ((g[:, at] - attn[:, at] * weights[...]) * inverses[...]).astype(BF16)
            e[:, at] = delta
            own[1, at] = dot(qt[at, :], delta, NN)
            if not mine:
                sib_message(1, j).start()
    sib_message(1, 2).start()
    start_first(1)
    for h in range(HEADS_HERE):
        normed[:, head(h)] = (attn[:, head(h)] * inverses[...] * gain[h : h + 1, :]).astype(BF16)

    def outer(h, carry):
        at = pl.ds(pl.multiple_of(h * DK, DK), DK)
        for r in range(4):
            low, rest = pl.ds(r * DK, DK), ROWS - r * DK
            strip = causal(dot(v[low, at], e[pl.ds(r * DK, rest), at], NT), False)
            dk_part[low, at] = dot(strip, q[pl.ds(r * DK, rest), at], NN)
            dv_part[low, at] = dot(scores_t[h, low, pl.ds(r * DK, rest)], e[pl.ds(r * DK, rest), at], NN)
        return carry

    lax.fori_loop(0, HEADS_HERE, outer, 0)
    start_second(1)

    for mine in (True, False):
        for j in range(2):
            at = half_head(c if mine else 1 - c, j)
            back = halves(state(0, mine, j), 1)
            for r in range(4):
                low = pl.ds(r * DK, DK)
                eh = e[low, at]
                strip = causal(dot(eh, v[pl.ds(0, (r + 1) * DK), at], NT), True)
                total = dot(strip, k[pl.ds(0, (r + 1) * DK), at], NN)
                dq[low, at] = (total + dot(jnp.concatenate([eh, eh], axis=1), back, NT)).astype(BF16)
    start_third(1)
    for mine in (True, False):
        for j in range(2):
            at = half_head(c if mine else 1 - c, j)
            if mine:
                last_products(at, state(1, mine, j), k, v, dk_part, dv_part, dk, dv)
            else:
                wait_pref(1, j)
                later[pl.ds(j * DK, DK)] = state(1, mine, j)

    leave(1)
    wait_bytes(zrecv, zsend_sem)


def last_products(at, back, k, v, dk_part, dv_part, dk, dv):
    vh, kh = v[:, at], k[:, at]
    total = dk_part[:, at] + dot(jnp.concatenate([vh, vh], axis=1), halves(back, 1), NT)
    dk[:, at] = total.astype(BF16)
    total = dv_part[:, at] + dot(jnp.concatenate([kh, kh], axis=1), halves(back, 0), NN)
    dv[:, at] = total.astype(BF16)


def finish(
    normed, dq, dk_mine, dv_mine, dk_part, dv_part, later, k, v,
    normed_hbm, dq_hbm, dk_hbm, dv_hbm,
    dk, dv, store_sem,
):
    c = lax.axis_index("seq") % 2
    stores = []

    def store(src, dst):
        copy = pltpu.make_async_copy(src, dst, store_sem.at[len(stores)])
        copy.start()
        stores.append(copy)

    here = pl.ds(pl.multiple_of(256 * c, 256), 256)
    store(dk_mine.at[:, here], dk_hbm.at[:, here])
    store(dv_mine.at[:, here], dv_hbm.at[:, here])
    for part in range(2):
        rows = pl.ds(256 * part, 256)
        store(normed.at[rows], normed_hbm.at[rows])
        store(dq.at[rows], dq_hbm.at[rows])
    for j in range(2):
        at = pl.ds(pl.multiple_of((2 * (1 - c) + j) * DK, DK), DK)
        last_products(at, later[pl.ds(j * DK, DK)], k, v, dk_part, dv_part, dk, dv)
        store(dk.at[:, at], dk_hbm.at[:, at])
        store(dv.at[:, at], dv_hbm.at[:, at])
    for copy in stores:
        copy.wait()


def shards(queries, keys, values, gain, d_out):
    width = HEADS_HERE * DK
    block = pltpu.VMEM((ROWS, width), BF16)
    wide = pltpu.VMEM((ROWS, width), F32)
    states = pltpu.VMEM((256, DK), F32)
    in_hbm = pl.BlockSpec(memory_space=pltpu.HBM)
    in_vmem = pl.BlockSpec(memory_space=pltpu.VMEM)
    gain = gain.astype(F32).reshape(HEADS_HERE, DK)
    queries, keys, values, d_out = (
        pltpu.with_memory_space_constraint(array, pltpu.HBM) for array in (queries, keys, values, d_out)
    )
    partial = pl.pallas_call(
        body,
        out_shape=[block, block, block, block, wide, wide, states, block, block],
        in_specs=[in_hbm, in_hbm, in_hbm, in_vmem, in_hbm],
        out_specs=[in_vmem] * 9,
        scratch_shapes=[
            block, block,
            pltpu.VMEM((width, ROWS), BF16),
            pltpu.VMEM((HEADS_HERE, ROWS, ROWS), BF16),
            wide, wide, block, pltpu.VMEM((ROWS, DK), F32), pltpu.VMEM((ROWS, DK), F32),
            pltpu.VMEM((2, width, DK), F32),
            pltpu.VMEM((2, 2, 256, DK), F32),
            pltpu.VMEM((2, PIECES, 2, PART, DK), F32),
            pltpu.VMEM((2, PIECES, 2, 3, PART, DK), F32),
            pltpu.VMEM((2, PIECES, PART, DK), F32),
            pltpu.VMEM((2, PIECES, 2, PART, DK), F32),
            pltpu.VMEM((2, PIECES, PIECE, DK), F32),
            pltpu.VMEM((2, PIECES, 2, 3, PART, DK), F32),
            pltpu.VMEM((2, width, DK), F32),
            pltpu.VMEM((8, DK), F32),
            pltpu.VMEM((DEPTH - 1, 8, DK), F32),
            pltpu.SemaphoreType.DMA((6,)),
            pltpu.SemaphoreType.DMA((2, 4)),
            pltpu.SemaphoreType.DMA((2, 3)),
            pltpu.SemaphoreType.DMA((2, 2)),
            pltpu.SemaphoreType.DMA((2, 2, PIECES)),
            pltpu.SemaphoreType.DMA,
            pltpu.SemaphoreType.DMA,
            pltpu.SemaphoreType.REGULAR((3,)),
            pltpu.SemaphoreType.REGULAR,
        ],
        compiler_params=pltpu.CompilerParams(
            collective_id=0, has_side_effects=True, vmem_limit_bytes=32 * 1024 * 1024
        ),
        name="attention",
    )(queries, keys, values, gain, d_out)
    return pl.pallas_call(
        finish,
        out_shape=[jax.ShapeDtypeStruct((ROWS, width), BF16)] * 4,
        in_specs=[in_vmem] * 9,
        out_specs=[in_hbm] * 4,
        scratch_shapes=[block, block, pltpu.SemaphoreType.DMA((10,))],
        compiler_params=pltpu.CompilerParams(vmem_limit_bytes=16 * 1024 * 1024),
        name="finish",
    )(*[pltpu.with_memory_space_constraint(array, pltpu.VMEM) for array in partial])


def solution(mesh):
    in_specs = (P("seq", "head"), P("seq", "head"), P("seq", "head"), P("head"), P("seq", "head"))
    out_specs = (P("seq", "head"), P("seq", "head"), P("seq", "head"), P("seq", "head"))
    return jax.shard_map(shards, mesh=mesh, in_specs=in_specs, out_specs=out_specs, check_vma=False)
```

```python
import functools

import jax
import jax.numpy as jnp
from jax import lax
from jax.experimental import pallas as pl
from jax.experimental.pallas import tpu as pltpu
from jax.sharding import PartitionSpec as P

DK = 128
ROWS = 512
HEADS_HERE = 4
PIECES = 4
PIECE = 256 // PIECES
PART = PIECE // 2
FEATURES = 8192
SIDE = 4
DEPTH = 16
MESH = pl.DeviceIdType.MESH
F32 = jnp.float32
BF16 = jnp.bfloat16

NN = (((1,), (0,)), ((), ()))
NT = (((1,), (1,)), ((), ()))
TN = (((0,), (0,)), ((), ()))


def dot(left, right, dims):
    return lax.dot_general(left, right, dims, preferred_element_type=F32)


def head(h):
    return pl.ds(h * DK, DK)


def halves(state, axis):
    high = state.astype(BF16)
    low = (state - high.astype(F32)).astype(BF16)
    return jnp.concatenate([high, low], axis=axis)


def body(
    q_hbm, k_hbm, v_hbm, gain_hbm, d_hbm,
    normed, dq, dk, dv, dk_part, dv_part, later, k, v,
    q, d, gain,
    qt, scores_t, attn, g, e, inverses, weights,
    own, sib, chip, recv1, row, cols, local, recv2, pref,
    zsend, zrecv,
    load_sem, send_sem, sib_sem, pref_sem, plane_sem, zsend_sem, zrecv_sem, near_sem, plane_near_sem,
):
    s = lax.axis_index("seq")
    z = lax.axis_index("head")
    x, y, c = s // 8, (s // 2) % SIDE, s % 2
    sibling = (s + 1 - 2 * c, z)

    def along_y(step):
        return (x * 8 + ((y + step) % SIDE) * 2 + c, z)

    def along_x(step):
        return (((x + step) % SIDE) * 8 + y * 2 + c, z)

    def along_z(step):
        return (s, (z + step) % DEPTH)

    here, there = pl.ds(pl.multiple_of(256 * c, 256), 256), pl.ds(pl.multiple_of(256 - 256 * c, 256), 256)
    loads = [
        pltpu.make_async_copy(src, dst, load_sem.at[i])
        for i, (src, dst) in enumerate(
            (
                (k_hbm.at[:, there], k.at[:, there]),
                (v_hbm.at[:, there], v.at[:, there]),
                (k_hbm.at[:, here], k.at[:, here]),
                (v_hbm.at[:, here], v.at[:, here]),
                (q_hbm, q),
                (d_hbm, d),
                (gain_hbm, gain),
            )
        )
    ]
    barrier = pltpu.get_barrier_semaphore()
    partners = [sibling, along_z(1), along_z(DEPTH - 1)]
    partners += [along_y(1), along_y(SIDE - 1), along_x(1), along_x(SIDE - 1)]
    for partner in partners:
        pl.semaphore_signal(barrier, inc=1, device_id=partner, device_id_type=MESH)
    for load in loads[:4]:
        load.start()

    def tell(turn):
        for step in (2**turn, DEPTH - 2**turn):
            pl.semaphore_signal(near_sem.at[turn], inc=1, device_id=along_z(step), device_id_type=MESH)

    def hear(turn):
        pl.semaphore_wait(near_sem.at[turn], 2)

    def tell_plane():
        for device in (along_y(SIDE - 1), along_x(SIDE - 1)):
            pl.semaphore_signal(plane_near_sem, inc=1, device_id=device, device_id_type=MESH)

    def half_head(half, j):
        return pl.ds(pl.multiple_of((2 * half + j) * DK, DK), DK)

    def message(send, recv, src, dst, device):
        return pltpu.make_async_remote_copy(
            src_ref=src, dst_ref=dst, send_sem=send, recv_sem=recv, device_id=device, device_id_type=MESH
        )

    def wait_bytes(ref, sem):
        pltpu.make_async_copy(ref, ref, sem).wait()

    def sib_message(way, j):
        send, recv = send_sem.at[way, 0], sib_sem.at[way, j]
        if j == 2:
            return message(send, recv, own.at[way, pl.ds(256 * c, 256)], sib.at[way, 1], sibling)
        return message(send, recv, own.at[way, half_head(1 - c, j)], sib.at[way, 0, pl.ds(j * DK, DK)], sibling)

    def piece(half, i):
        return pl.ds(pl.multiple_of(256 * half + PIECE * i, PIECE), PIECE)

    def pref_message(way, j):
        at = half_head(c, j)
        return message(send_sem.at[way, 1], pref_sem.at[way, j], pref.at[way, at], pref.at[way, at], sibling)

    def plane_message(way, phase, i, a, step):
        device = along_y(step) if phase == a else along_x(step)
        if phase == 0:
            src, dst = chip.at[way, i, a], recv1.at[way, i, a, step - 1]
        elif a == 0:
            src, dst = row.at[way, i], recv2.at[way, i, a, step - 1]
        else:
            wrapped = (y + step) // SIDE
            pick = 1 - wrapped if way == 0 else wrapped
            src, dst = cols.at[way, i, pick], recv2.at[way, i, a, step - 1]
        return message(send_sem.at[way, 2 + phase], plane_sem.at[way, phase, i], src, dst, device)

    def zmessage(step):
        return message(zsend_sem, zrecv_sem, zsend, zrecv.at[step - 1], along_z(step))

    def counts(way, step, place):
        return step <= place if way == 0 else step > place

    def start_plane(way, phase, i):
        for step in (2, 1, 3):
            for a in range(2):
                plane_message(way, phase, i, a, step).start()

    def start_first(way):
        for i in range(PIECES):
            if i % (PIECES // 2) == 0:
                sib_message(way, i // (PIECES // 2)).wait_recv()
            total = own[way, piece(c, i)] + sib[way, 0, pl.ds(PIECE * i, PIECE)]
            for a in range(2):
                chip[way, i, a] = total[PART * a : PART * a + PART]
            start_plane(way, 0, i)

    def start_second(way):
        for i in range(PIECES):
            wait_bytes(recv1.at[way, i], plane_sem.at[way, 0, i])
            total, before = chip[way, i, 0], jnp.zeros((PART, DK), F32)
            column = jnp.zeros((PART, DK), F32)
            for step in range(1, SIDE):
                total = total + recv1[way, i, 0, step - 1]
                column = column + jnp.where(counts(way, step, x), recv1[way, i, 1, step - 1], 0.0)
            row[way, i] = total
            cols[way, i, 0] = column
            cols[way, i, 1] = column + chip[way, i, 1]
            start_plane(way, 1, i)
            for step in range(1, SIDE):
                before = before + jnp.where(counts(way, step, y), recv1[way, i, 0, step - 1], 0.0)
            local[way, i, pl.ds(0, PART)] = before
            local[way, i, pl.ds(PART, PART)] = column

    def start_third(way):
        sib_message(way, 2).wait_recv()
        for i in range(PIECES):
            wait_bytes(recv2.at[way, i], plane_sem.at[way, 1, i])
            first = local[way, i, pl.ds(0, PART)]
            second = local[way, i, pl.ds(PART, PART)]
            for step in range(1, SIDE):
                first = first + jnp.where(counts(way, step, x), recv2[way, i, 0, step - 1], 0.0)
                second = second + recv2[way, i, 1, step - 1]
            pref[way, piece(c, i)] = jnp.concatenate([first, second], axis=0)
            if (i + 1) % (PIECES // 2) == 0:
                pref_message(way, i // (PIECES // 2)).start()

    def wait_pref(way, j):
        wait_bytes(pref.at[way, half_head(1 - c, j)], pref_sem.at[way, j])

    def leave(way):
        wait_bytes(own.at[way], send_sem.at[way, 0])
        wait_bytes(pref.at[way, pl.ds(0, 256)], send_sem.at[way, 1])
        wait_bytes(recv1.at[way], send_sem.at[way, 2])
        wait_bytes(recv2.at[way], send_sem.at[way, 3])

    def state(way, mine, j):
        add = c == 1 if way == 0 else c == 0
        block = sib[way, 0 if mine else 1, pl.ds(j * DK, DK)]
        return pref[way, half_head(c if mine else 1 - c, j)] + jnp.where(add, block, 0.0)

    steps0 = lax.broadcasted_iota(jnp.int32, (DK, DK), 0)
    steps1 = lax.broadcasted_iota(jnp.int32, (DK, DK), 1)

    def causal(block, lower):
        keep = steps0 >= steps1 if lower else steps0 <= steps1
        if block.shape[1] == DK:
            return jnp.where(keep, block, 0.0).astype(BF16)
        if lower:
            cut = block.shape[1] - DK
            return jnp.concatenate(
                [block[:, :cut].astype(BF16), jnp.where(keep, block[:, cut:], 0.0).astype(BF16)], axis=1
            )
        return jnp.concatenate(
            [jnp.where(keep, block[:, :DK], 0.0).astype(BF16), block[:, DK:].astype(BF16)], axis=1
        )

    for load in loads[:2]:
        load.wait()
    for load in loads[4:]:
        load.start()
    for j in range(2):
        at = half_head(1 - c, j)
        own[0, at] = dot(k[:, at], v[:, at], TN)
    pl.semaphore_wait(barrier, len(partners))
    tell_plane()
    tell(0)
    for j in range(2):
        sib_message(0, j).start()
    for load in loads[2:4]:
        load.wait()
    for j in range(2):
        at = half_head(c, j)
        own[0, at] = dot(k[:, at], v[:, at], TN)
    sib_message(0, 2).start()
    pl.semaphore_wait(plane_near_sem, 2)
    start_first(0)
    for load in loads[4:]:
        load.wait()

    def inner(h, carry):
        at = pl.ds(pl.multiple_of(h * DK, DK), DK)
        for r in range(4):
            strip = causal(dot(q[pl.ds(r * DK, DK), at], k[pl.ds(0, (r + 1) * DK), at], NT), True)
            attn[pl.ds(r * DK, DK), at] = dot(strip, v[pl.ds(0, (r + 1) * DK), at], NN)
        return carry

    lax.fori_loop(0, HEADS_HERE, inner, 0)
    hear(0)
    tell(1)
    start_second(0)

    def prepare(h, carry):
        at = pl.ds(pl.multiple_of(h * DK, DK), DK)
        qt[at, :] = q[:, at].astype(F32).T.astype(BF16)
        for r in range(4):
            rest = ROWS - r * DK
            strip = dot(k[pl.ds(r * DK, DK), at], q[pl.ds(r * DK, rest), at], NT)
            scores_t[h, pl.ds(r * DK, DK), pl.ds(r * DK, rest)] = causal(strip, False)
        return carry

    lax.fori_loop(0, HEADS_HERE, prepare, 0)
    for h in range(HEADS_HERE):
        g[:, head(h)] = d[:, head(h)].astype(F32) * gain[h : h + 1, :].astype(F32)
    hear(1)
    tell(2)
    start_third(0)

    squares = jnp.zeros((ROWS, DK), F32)
    products = jnp.zeros((ROWS, DK), F32)
    for mine in (True, False):
        for j in range(2):
            if not mine:
                wait_pref(0, j)
            at = half_head(c if mine else 1 - c, j)
            qh = q[:, at]
            total = attn[:, at] + dot(jnp.concatenate([qh, qh], axis=1), halves(state(0, mine, j), 0), NN)
            attn[:, at] = total
            squares = squares + total * total
            products = products + total * g[:, at]

    ones = jnp.ones((8, 3 * DK), BF16)

    def row_sums(array):
        high = array.astype(BF16)
        rest = array - high.astype(F32)
        middle = rest.astype(BF16)
        low = (rest - middle.astype(F32)).astype(BF16)
        return dot(ones, jnp.concatenate([high, middle, low], axis=1), NT)

    for i, array in enumerate((squares, products)):
        sums = row_sums(array)
        for j in range(4):
            zsend[pl.ds(4 * i + j, 1), :] = sums[0:1, j * DK : (j + 1) * DK]
    hear(2)
    for step in (8, 7, 9, 6, 10, 5, 11, 4, 12, 3, 13, 2, 14, 1, 15):
        zmessage(step).start()

    leave(0)
    wait_bytes(zrecv, zrecv_sem)
    totals = zsend[...]
    for step in range(1, DEPTH):
        totals = totals + zrecv[step - 1]
    means = totals / FEATURES
    rms = jnp.sqrt(means[0:4] + 1e-05)
    inverse = 1.0 / rms
    weight = means[4:8] * inverse * inverse
    columns = jnp.concatenate([inverse, weight], axis=0).T
    for j in range(4):
        inverses[pl.ds(j * DK, DK), :] = jnp.broadcast_to(columns[:, j : j + 1], (DK, DK))
        weights[pl.ds(j * DK, DK), :] = jnp.broadcast_to(columns[:, 4 + j : 5 + j], (DK, DK))
    for mine in (False, True):
        for j in range(2):
            at = half_head(c if mine else 1 - c, j)
            delta = ((g[:, at] - attn[:, at] * weights[...]) * inverses[...]).astype(BF16)
            e[:, at] = delta
            own[1, at] = dot(qt[at, :], delta, NN)
            if not mine:
                sib_message(1, j).start()
    sib_message(1, 2).start()
    start_first(1)
    for h in range(HEADS_HERE):
        normed[:, head(h)] = (attn[:, head(h)] * inverses[...] * gain[h : h + 1, :].astype(F32)).astype(BF16)

    def outer(h, carry):
        at = pl.ds(pl.multiple_of(h * DK, DK), DK)
        for r in range(4):
            low, rest = pl.ds(r * DK, DK), ROWS - r * DK
            strip = causal(dot(v[low, at], e[pl.ds(r * DK, rest), at], NT), False)
            dk_part[low, at] = dot(strip, q[pl.ds(r * DK, rest), at], NN)
            dv_part[low, at] = dot(scores_t[h, low, pl.ds(r * DK, rest)], e[pl.ds(r * DK, rest), at], NN)
        return carry

    lax.fori_loop(0, HEADS_HERE, outer, 0)
    start_second(1)

    for mine in (True, False):
        for j in range(2):
            at = half_head(c if mine else 1 - c, j)
            back = halves(state(0, mine, j), 1)
            for r in range(4):
                low = pl.ds(r * DK, DK)
                eh = e[low, at]
                strip = causal(dot(eh, v[pl.ds(0, (r + 1) * DK), at], NT), True)
                total = dot(strip, k[pl.ds(0, (r + 1) * DK), at], NN)
                dq[low, at] = (total + dot(jnp.concatenate([eh, eh], axis=1), back, NT)).astype(BF16)
    start_third(1)
    for mine in (True, False):
        for j in range(2):
            at = half_head(c if mine else 1 - c, j)
            if mine:
                last_products(at, state(1, mine, j), k, v, dk_part, dv_part, dk, dv)
            else:
                wait_pref(1, j)
                later[pl.ds(j * DK, DK)] = state(1, mine, j)

    leave(1)
    wait_bytes(zrecv, zsend_sem)


def last_products(at, back, k, v, dk_part, dv_part, dk, dv):
    vh, kh = v[:, at], k[:, at]
    total = dk_part[:, at] + dot(jnp.concatenate([vh, vh], axis=1), halves(back, 1), NT)
    dk[:, at] = total.astype(BF16)
    total = dv_part[:, at] + dot(jnp.concatenate([kh, kh], axis=1), halves(back, 0), NN)
    dv[:, at] = total.astype(BF16)


def finish(
    normed, dq, dk_mine, dv_mine, dk_part, dv_part, later, k, v,
    normed_hbm, dq_hbm, dk_hbm, dv_hbm,
    dk, dv, store_sem,
):
    c = lax.axis_index("seq") % 2
    stores = []

    def store(src, dst):
        copy = pltpu.make_async_copy(src, dst, store_sem.at[len(stores)])
        copy.start()
        stores.append(copy)

    here = pl.ds(pl.multiple_of(256 * c, 256), 256)
    store(dk_mine.at[:, here], dk_hbm.at[:, here])
    store(dv_mine.at[:, here], dv_hbm.at[:, here])
    for part in range(2):
        rows = pl.ds(256 * part, 256)
        store(normed.at[rows], normed_hbm.at[rows])
        store(dq.at[rows], dq_hbm.at[rows])
    for j in range(2):
        at = pl.ds(pl.multiple_of((2 * (1 - c) + j) * DK, DK), DK)
        last_products(at, later[pl.ds(j * DK, DK)], k, v, dk_part, dv_part, dk, dv)
        store(dk.at[:, at], dk_hbm.at[:, at])
        store(dv.at[:, at], dv_hbm.at[:, at])
    for copy in stores:
        copy.wait()


def shards(queries, keys, values, gain, d_out):
    width = HEADS_HERE * DK
    block = pltpu.VMEM((ROWS, width), BF16)
    wide = pltpu.VMEM((ROWS, width), F32)
    states = pltpu.VMEM((256, DK), F32)
    in_hbm = pl.BlockSpec(memory_space=pltpu.HBM)
    in_vmem = pl.BlockSpec(memory_space=pltpu.VMEM)
    arguments = (queries, keys, values, gain.reshape(HEADS_HERE, DK), d_out)
    partial = pl.pallas_call(
        body,
        out_shape=[block, block, block, block, wide, wide, states, block, block],
        in_specs=[in_hbm] * 5,
        out_specs=[in_vmem] * 9,
        scratch_shapes=[
            block, block, pltpu.VMEM((HEADS_HERE, DK), BF16),
            pltpu.VMEM((width, ROWS), BF16),
            pltpu.VMEM((HEADS_HERE, ROWS, ROWS), BF16),
            wide, wide, block, pltpu.VMEM((ROWS, DK), F32), pltpu.VMEM((ROWS, DK), F32),
            pltpu.VMEM((2, width, DK), F32),
            pltpu.VMEM((2, 2, 256, DK), F32),
            pltpu.VMEM((2, PIECES, 2, PART, DK), F32),
            pltpu.VMEM((2, PIECES, 2, 3, PART, DK), F32),
            pltpu.VMEM((2, PIECES, PART, DK), F32),
            pltpu.VMEM((2, PIECES, 2, PART, DK), F32),
            pltpu.VMEM((2, PIECES, PIECE, DK), F32),
            pltpu.VMEM((2, PIECES, 2, 3, PART, DK), F32),
            pltpu.VMEM((2, width, DK), F32),
            pltpu.VMEM((8, DK), F32),
            pltpu.VMEM((DEPTH - 1, 8, DK), F32),
            pltpu.SemaphoreType.DMA((7,)),
            pltpu.SemaphoreType.DMA((2, 4)),
            pltpu.SemaphoreType.DMA((2, 3)),
            pltpu.SemaphoreType.DMA((2, 2)),
            pltpu.SemaphoreType.DMA((2, 2, PIECES)),
            pltpu.SemaphoreType.DMA,
            pltpu.SemaphoreType.DMA,
            pltpu.SemaphoreType.REGULAR((3,)),
            pltpu.SemaphoreType.REGULAR,
        ],
        compiler_params=pltpu.CompilerParams(
            collective_id=0, has_side_effects=True, vmem_limit_bytes=32 * 1024 * 1024
        ),
        name="attention",
    )(*[pltpu.with_memory_space_constraint(array, pltpu.HBM) for array in arguments])
    return pl.pallas_call(
        finish,
        out_shape=[jax.ShapeDtypeStruct((ROWS, width), BF16)] * 4,
        in_specs=[in_vmem] * 9,
        out_specs=[in_hbm] * 4,
        scratch_shapes=[block, block, pltpu.SemaphoreType.DMA((10,))],
        compiler_params=pltpu.CompilerParams(vmem_limit_bytes=16 * 1024 * 1024),
        name="finish",
    )(*[pltpu.with_memory_space_constraint(array, pltpu.VMEM) for array in partial])


def solution(mesh):
    in_specs = (P("seq", "head"), P("seq", "head"), P("seq", "head"), P("head"), P("seq", "head"))
    out_specs = (P("seq", "head"), P("seq", "head"), P("seq", "head"), P("seq", "head"))
    return jax.shard_map(shards, mesh=mesh, in_specs=in_specs, out_specs=out_specs, check_vma=False)
```
